512 devices in a mesh: pack: 32 (over x, z), seq: 16 (over y, core).
Axes of the slice: x: 4, y: 8, z: 8, core: 2. Of those that a mesh axis runs over, the one named last changes fastest.
Arguments:
- source: bfloat16 [16, 6144, 1152], P('seq', 'pack')
- destination: int32 [16, 6144], P('seq', 'pack'), may hold values from 0 to 6143, as said below
- doc_ids: int32 [32, 3072], P('pack'), may hold values from 0 to 23, as said below
- w_qkv: bfloat16 [3, 1152, 1152], P(None, None, 'seq')
- w_out: bfloat16 [1152, 1152], P('seq'), may hold values from -0.1875 to 0.1875
Outputs:
- projected: bfloat16 [32, 3072, 1152], P('pack', 'seq')
The draws below stay inside these ranges and needn't reach their ends.
Inputs may be any that keep to these rules, and one draw needn't show every extreme that they name: For every column s, destination[s] is a permutation of 0 to 6143. Of the 192 rows of one device, at most 12 have the same destination // 192, and in every column some device sends exactly 12 rows to one owner. doc_ids[p] starts at 0, never falls, rises by one at most from one position to the next and changes only at positions that are multiples of 128; some packed row reaches the largest value.
All inputs are finite; a program needn't handle non-finite values.
Results may differ from the reference program's by a relative error of at most 0.011.
Values may be sent and summed in bfloat16 or wider, within the bound.
No kernel may reach another device: no remote copies, remote signals or barrier semaphores. Data moves between devices by JAX's collectives and lax.ppermute only.
A program may use at most 64 MiB of HBM per device.

```python
import math
import jax
import jax.numpy as jnp
from jax import lax

D = 1152
H = 16
HD = 72
TOK_DEV = 192
DOC_BLOCK = 128
ROW_LEN = 3072
N_PACK = 32
N_SEQ = 16


def draw_destination(key, part):
    key = jax.random.fold_in(key, 11)
    first, second, third = jax.random.split(key, 3)
    base = TOK_DEV // N_PACK
    excess = jax.random.randint(first, (N_SEQ, N_PACK), 0, base + 1)
    excess = excess.at[:, 0].set(base).at[:, 1].set(0)
    counts = base + excess - jnp.roll(excess, -1, axis=1)
    ends = jnp.cumsum(counts, axis=1)
    keys_one = jax.random.split(second, N_SEQ * N_PACK)
    ranks = jax.vmap(lambda single: jax.random.permutation(single, TOK_DEV))(keys_one).reshape(N_SEQ, N_PACK, TOK_DEV)
    keys_two = jax.random.split(third, N_SEQ * N_PACK)
    arrival = jax.vmap(lambda single: jax.random.permutation(single, TOK_DEV))(keys_two).reshape(N_SEQ, N_PACK * TOK_DEV)
    offset = jnp.sum(ranks[..., None] >= ends[:, None, None, :], axis=-1).astype(jnp.int32)
    sender = jnp.arange(N_PACK, dtype=jnp.int32)[None, :, None]
    owner = (sender + offset) % N_PACK
    lookup = (owner * TOK_DEV + ranks).reshape(N_SEQ, N_PACK * TOK_DEV)
    places = jnp.take_along_axis(arrival, lookup, axis=1)
    return (owner.reshape(N_SEQ, N_PACK * TOK_DEV) * TOK_DEV + places).astype(jnp.int32)


def draw_doc_ids(key, part):
    key = jax.random.fold_in(key, 13)
    blocks = ROW_LEN // DOC_BLOCK
    starts = (jax.random.randint(key, (N_PACK, blocks), 0, 4) == 0).astype(jnp.int32)
    starts = starts.at[0, :].set(1)
    starts = starts.at[:, 0].set(0)
    numbers = jnp.cumsum(starts, axis=1)
    return jnp.repeat(numbers, DOC_BLOCK, axis=1).astype(jnp.int32)


def draw_source(key, part):
    key = jax.random.fold_in(key, 5)
    first = jax.random.fold_in(key, 0)
    shape = (N_SEQ, N_PACK * TOK_DEV, D)
    values = jax.random.normal(first, shape, jnp.float32)
    return values.astype(jnp.bfloat16)


def draw_w_qkv(key, part):
    key = jax.random.fold_in(key, 7)
    first, second, third = jax.random.split(key, 3)
    shape = (D, D)
    query_w = jax.random.normal(first, shape, jnp.float32)
    key_w = jax.random.normal(second, shape, jnp.float32)
    value_w = jax.random.normal(third, shape, jnp.float32)
    return (jnp.stack([query_w, key_w, value_w]) * D ** (-0.5)).astype(jnp.bfloat16)


def levels(key, dims, cuts, low, largest):
    gain = 1.0
    for axis_at, parts in cuts:
        steps = jax.random.uniform(jax.random.fold_in(jax.random.fold_in(key, 6), axis_at), (parts,), jnp.float32, low / len(cuts), largest / len(cuts))
        gain = gain * jnp.repeat(jnp.exp(steps), dims[axis_at] // parts).reshape((-1,) + (1,) * (len(dims) - 1 - axis_at))
    return gain


def centred(own_key, shape, deviation, reach, cuts=(), kind=jnp.bfloat16):
    gain = levels(own_key, shape, cuts, -0.22, 0.18) if cuts else 1.0
    result = jax.random.normal(own_key, shape, jnp.float32) * deviation * gain
    return jnp.minimum(jnp.maximum(result, -reach), reach).astype(kind)


def setup_inputs(seed: int = 0) -> dict:
    keys = jax.random.split(jax.random.key(seed), 6)
    return {
        "source": draw_source(jax.random.fold_in(keys[5], 71), 0),
        "destination": draw_destination(jax.random.fold_in(keys[5], 71), 0),
        "doc_ids": draw_doc_ids(jax.random.fold_in(keys[5], 71), 0),
        "w_qkv": draw_w_qkv(jax.random.fold_in(keys[5], 71), 0),
        "w_out": centred(keys[4], (D, D), D ** -0.5, 0.1875, ((0, 16),)),
    }


def attend_head(queries, key_rows, value_rows, same_doc):
    scores = jnp.dot(queries, key_rows.T, preferred_element_type=jnp.float32) / math.sqrt(HD)
    scores = jnp.where(same_doc, scores, -jnp.inf)
    highest = lax.optimization_barrier(jnp.max(scores, axis=1, keepdims=True))
    expo = jnp.exp(scores - highest)
    weights = (expo / lax.optimization_barrier(jnp.sum(expo, axis=1, keepdims=True))).astype(jnp.bfloat16)
    return jnp.dot(weights, value_rows, preferred_element_type=jnp.float32).astype(jnp.bfloat16)

def reference(source, destination, doc_ids, w_qkv, w_out):
    column = jnp.arange(N_SEQ, dtype=jnp.int32)[:, None]
    target = destination // TOK_DEV * ROW_LEN + column * TOK_DEV + destination % TOK_DEV
    packed = jnp.zeros((N_PACK * ROW_LEN, D), jnp.bfloat16)
    packed = packed.at[target.reshape(-1)].set(source.reshape(-1, D)).reshape(N_PACK, ROW_LEN, D)

    def one_row(inputs):
        tokens, documents = inputs
        stacked = jnp.stack([jnp.dot(tokens, w_qkv[which], preferred_element_type=jnp.float32) for which in range(3)]).astype(jnp.bfloat16)
        by_head = stacked.reshape(3, ROW_LEN, H, HD).transpose(2, 0, 1, 3)
        same_doc = documents[:, None] == documents[None, :]
        heads_out = lax.map(lambda grouped: attend_head(grouped[0], grouped[1], grouped[2], same_doc), by_head)
        merged = heads_out.transpose(1, 0, 2).reshape(ROW_LEN, D)
        return jnp.dot(merged, w_out, preferred_element_type=jnp.float32).astype(jnp.bfloat16)
    return lax.map(one_row, (packed, doc_ids))
```

```python
import functools
import math

import jax
import jax.numpy as jnp
from jax import lax
from jax.experimental import pallas as pl
from jax.experimental.pallas import tpu as pltpu
from jax.sharding import PartitionSpec as P

HD = 72
CAP = 12
LANES = 128
BLK = 128
BF = jnp.bfloat16
F32 = jnp.float32
NT = (((1,), (1,)), ((), ()))

SHIFTS = (
    (0, ((0, 0), (3, 4), (6, 8))),
    (-12, ((0, 1), (3, 5))),
    (4, ((1, 1), (4, 5))),
    (-8, ((1, 2), (4, 6))),
    (8, ((2, 2), (5, 6))),
    (-4, ((2, 3), (5, 7))),
)
TILES = 7


def iota(shape, dim):
    return lax.broadcasted_iota(jnp.int32, shape, dim)


def onehot(condition):
    return jnp.where(condition, 1.0, 0.0).astype(BF)


def pack_kernel(n_pack, dest_ref, rows_ref, out_ref):
    tok = rows_ref.shape[0]
    group = n_pack * 16
    dest = dest_ref[...]
    owner = ((dest >> 6) * 171) >> 9
    place = dest - owner * tok
    owned = iota((n_pack, tok), 0) == owner
    before = onehot(iota((tok, tok), 0) < iota((tok, tok), 1))
    counted = jnp.dot(onehot(owned), before, preferred_element_type=F32)
    slot = jnp.sum(jnp.where(owned, counted, 0.0), axis=0, keepdims=True).astype(jnp.int32)
    row = iota((group, tok), 0)
    parts = {}
    for shift, pairs in SHIFTS:
        at = slot - shift
        key = jnp.where((at >= 0) & (at < 16), owner * 16 + at, -1)
        picked = jnp.concatenate(
            [rows_ref[:, f * LANES : (f + 1) * LANES] for _, f in pairs], axis=1
        )
        moved = jnp.dot(onehot(row == key), picked, preferred_element_type=F32)
        for n, (tile, _) in enumerate(pairs):
            parts.setdefault(tile, []).append(moved[:, n * LANES : (n + 1) * LANES])
    tags = jnp.where(iota((LANES, tok), 0) == slot, (place + 1).astype(F32), 0.0).astype(BF)
    here = onehot(row == owner * 16 + CAP)
    parts[TILES - 1].append(lax.dot_general(here, tags, NT, preferred_element_type=F32))
    for tile in range(TILES):
        whole = functools.reduce(lambda a, b: a + b, parts[tile])
        out_ref[:, tile * 16 : (tile + 1) * 16, :] = whole.astype(BF).reshape(n_pack, 16, LANES)


def unpack_kernel(n_pack, in_ref, out_ref):
    tok = out_ref.shape[0]
    group = n_pack * 16
    tiles = [in_ref[:, t * 16 : (t + 1) * 16, :].reshape(group, LANES) for t in range(TILES)]
    col = iota((n_pack, group), 1)
    lead = iota((n_pack, group), 0) * 16
    labels = jnp.dot(onehot(col == lead + CAP), tiles[-1], preferred_element_type=F32).astype(BF)
    mine = (col >= lead) & (col < lead + 16)
    offset = iota((LANES, group), 0) - (iota((LANES, group), 1) & 15)
    place = iota((tok, group), 0) + 1
    parts = {}
    for shift, pairs in SHIFTS:
        spread = jnp.dot(labels, onehot(offset == shift), preferred_element_type=F32)
        label = jnp.sum(jnp.where(mine, spread, 0.0), axis=0, keepdims=True).astype(jnp.int32)
        picked = jnp.concatenate([tiles[t] for t, _ in pairs], axis=1)
        moved = jnp.dot(onehot(place == label), picked, preferred_element_type=F32)
        for n, (_, f) in enumerate(pairs):
            parts.setdefault(f, []).append(moved[:, n * LANES : (n + 1) * LANES])
    for f in sorted(parts):
        whole = functools.reduce(lambda a, b: a + b, parts[f])
        out_ref[:, f * LANES : (f + 1) * LANES] = whole.astype(BF)


TOKT = 256
QT = 256
KT = 512
AROWS = 112
NEG = -3e38
LIMIT = pltpu.CompilerParams(vmem_limit_bytes=56 * 2**20)


def attend_kernel(steps, n_seq, doc_ref, x_ref, w_ref, out_ref, q_s, k_s, v_s, o_s, bound_s):
    step = pl.program_id(0)
    rows = pl.ds(pl.multiple_of(step * TOKT, TOKT), TOKT)
    x = x_ref[...]
    qkv = [
        lax.dot_general(x, w_ref[j], NT, preferred_element_type=F32).astype(BF) for j in range(3)
    ]
    q_s[rows, :] = qkv[0]
    k_s[rows, :] = qkv[1]
    v_s[rows, 0:HD] = qkv[2]
    v_s[rows, HD:LANES] = jnp.where(iota((TOKT, LANES - HD), 1) == 0, 1.0, 0.0).astype(BF)

    @pl.when(step == steps - 1)
    def _():
        length = k_s.shape[0] - KT
        blocks = length // BLK
        scale = math.log2(math.e) / math.sqrt(HD)
        k_s[length:, :] = jnp.zeros((KT, HD), BF)
        v_s[length:, :] = jnp.zeros((KT, LANES), BF)
        first = jnp.int32(0)
        for b in range(blocks):
            if b:
                first = jnp.where(doc_ref[0, b * BLK] == doc_ref[0, (b - 1) * BLK], first, b)
            bound_s[0, b] = first
        last = jnp.int32(blocks)
        for b in reversed(range(blocks)):
            if b < blocks - 1:
                last = jnp.where(doc_ref[0, b * BLK] == doc_ref[0, (b + 1) * BLK], last, b + 1)
            bound_s[1, b] = last
        per = QT // BLK

        def one_tile(t, _):
            q = q_s[pl.ds(pl.multiple_of(t * QT, QT), QT), :]
            lo = bound_s[0, t * per]
            hi = bound_s[1, t * per + per - 1]
            chunks = (hi - lo + KT // BLK - 1) // (KT // BLK)

            def one_chunk(c, carry):
                high, total = carry
                begin = lo + c * (KT // BLK)
                keys = pl.ds(pl.multiple_of(begin * BLK, BLK), KT)
                scores = lax.dot_general(q, k_s[keys, :], NT, preferred_element_type=F32)
                block = begin + iota((1, KT), 1) // BLK
                halves = []
                for i in range(per):
                    keep = (block >= bound_s[0, t * per + i]) & (block < bound_s[1, t * per + i])
                    halves.append(
                        jnp.where(keep, scores[i * BLK : (i + 1) * BLK, :], -jnp.inf)
                    )
                scores = jnp.concatenate(halves, axis=0)
                newer = jnp.maximum(high, jnp.max(scores, axis=1, keepdims=True))
                expo = jnp.exp2((scores - newer) * scale).astype(BF)
                total = total * jnp.exp2((high - newer) * scale) + jnp.dot(
                    expo, v_s[keys, :], preferred_element_type=F32
                )
                return newer, total

            high = jnp.full((QT, 1), NEG, F32)
            total = jnp.zeros((QT, LANES), F32)
            _, total = lax.fori_loop(0, chunks, one_chunk, (high, total))
            done = total[:, 0:HD] / total[:, HD : HD + 1]
            o_s[pl.ds(pl.multiple_of(t * QT, QT), QT), 0:HD] = done
            return 0

        lax.fori_loop(0, length // QT, one_tile, 0)
        tok = length // n_seq
        for s in range(n_seq):
            turned = o_s[s * tok : (s + 1) * tok, :].T
            out_ref[s, 0:64, :] = turned[0:64, 0:LANES].astype(BF)
            out_ref[s, 64:96, :] = jnp.concatenate(
                [turned[0:32, LANES:tok], turned[32:64, LANES:tok]], axis=1
            ).astype(BF)
            out_ref[s, 96:112, :] = jnp.concatenate(
                [
                    turned[64:72, 0:LANES],
                    jnp.concatenate(
                        [turned[64:72, LANES:tok], jnp.zeros((8, 2 * LANES - tok), F32)], axis=1
                    ),
                ],
                axis=0,
            ).astype(BF)


def project_kernel(n_seq, in_ref, w_ref, out_ref):
    width = out_ref.shape[1]
    tok = out_ref.shape[0]
    rest = tok - LANES
    lo = in_ref[:, 0:32, :].reshape(n_seq * 32, LANES)
    hi = in_ref[:, 32:64, :].reshape(n_seq * 32, LANES)
    far = in_ref[:, 64:96, :].reshape(n_seq * 32, LANES)
    tail = in_ref[:, 96:112, :].reshape(n_seq * 16, LANES).astype(F32)
    upper = (iota(tail.shape, 0) & 15) < 8
    tail_near = jnp.where(upper, tail, 0.0).astype(BF)
    tail_far = jnp.where(upper, 0.0, tail).astype(BF)
    near = jnp.concatenate([lo, hi, tail_near], axis=0).T
    far_t = far.T
    distant = jnp.concatenate([far_t[0:rest], far_t[rest:LANES], tail_far.T[0:rest]], axis=1)
    left = jnp.concatenate([near, distant], axis=0)
    weights = jnp.concatenate(
        [
            w_ref[:, 0:32, :].reshape(n_seq * 32, width),
            w_ref[:, 32:64, :].reshape(n_seq * 32, width),
            w_ref[:, 64:80, :].reshape(n_seq * 16, width),
        ],
        axis=0,
    )
    out_ref[...] = jnp.dot(left, weights, preferred_element_type=F32).astype(BF)


def whole(*shape):
    return pl.BlockSpec(shape, lambda *_: (0,) * len(shape))


def attend_call(doc_ids, tokens, w_t, n_seq):
    length, width = tokens.shape
    steps = length // TOKT
    return pl.pallas_call(
        functools.partial(attend_kernel, steps, n_seq),
        grid=(steps,),
        out_shape=jax.ShapeDtypeStruct((n_seq, AROWS, LANES), BF),
        in_specs=[
            pl.BlockSpec(memory_space=pltpu.SMEM),
            pl.BlockSpec((TOKT, width), lambda i: (i, 0)),
            whole(3, HD, width),
        ],
        out_specs=whole(n_seq, AROWS, LANES),
        scratch_shapes=[
            pltpu.VMEM((length, HD), BF),
            pltpu.VMEM((length + KT, HD), BF),
            pltpu.VMEM((length + KT, LANES), BF),
            pltpu.VMEM((length, LANES), F32),
            pltpu.SMEM((2, length // BLK), jnp.int32),
        ],
        compiler_params=LIMIT,
        name="attend",
    )(doc_ids, tokens, w_t)


def body(source, destination, doc_ids, w_qkv, w_out):
    n_pack = lax.axis_size("pack")
    n_seq = lax.axis_size("seq")
    tok, width = source.shape[1:]
    spare = jnp.concatenate([w_out, w_out[64:HD]], axis=0)
    w_all = lax.all_gather(spare, "seq", axis=0, tiled=False)

    outbox = pl.pallas_call(
        functools.partial(pack_kernel, n_pack),
        out_shape=jax.ShapeDtypeStruct((n_pack, TILES * 16, LANES), BF),
        compiler_params=LIMIT,
        name="pack_rows",
    )(destination, source[0])
    inbox = lax.all_to_all(outbox, "pack", split_axis=0, concat_axis=0, tiled=True)
    packed = pl.pallas_call(
        functools.partial(unpack_kernel, n_pack),
        out_shape=jax.ShapeDtypeStruct((tok, width), BF),
        compiler_params=LIMIT,
        name="unpack_rows",
    )(inbox)
    tokens = lax.all_gather(packed, "seq", axis=0, tiled=True)

    attended = attend_call(doc_ids, tokens, jnp.transpose(w_qkv, (0, 2, 1)), n_seq)
    blocks = lax.all_to_all(attended, "seq", split_axis=0, concat_axis=0, tiled=True)

    out = pl.pallas_call(
        functools.partial(project_kernel, n_seq),
        out_shape=jax.ShapeDtypeStruct((tok, width), BF),
        compiler_params=LIMIT,
        name="project",
    )(blocks, w_all)
    return out[None]


def solution(mesh):
    placed = (
        P("seq", "pack", None),
        P("seq", "pack"),
        P("pack", None),
        P(None, None, "seq"),
        P("seq", None),
    )
    return jax.shard_map(
        body, mesh=mesh, in_specs=placed, out_specs=P("pack", "seq", None), check_vma=False
    )
```

```python
import functools
import math

import jax
import jax.numpy as jnp
from jax import lax
from jax.experimental import pallas as pl
from jax.experimental.pallas import tpu as pltpu
from jax.sharding import PartitionSpec as P

HD = 72
TOK = 192
CAP = 12
LANES = 128
BLK = 128
BF = jnp.bfloat16
F32 = jnp.float32
NT = (((1,), (1,)), ((), ()))

NEAR = 5
FAR = 4


def tile_shifts(chunks):
    found = {}
    for f in range(chunks):
        for t in range(CAP * f // 16, (CAP * f + CAP - 1) // 16 + 1):
            found.setdefault(16 * t - CAP * f, []).append((t, f))
    return found


def iota(shape, dim):
    return lax.broadcasted_iota(jnp.int32, shape, dim)


def onehot(condition):
    return jnp.where(condition, 1.0, 0.0).astype(BF)


def slots_of(dest, n_pack, tok):
    owner = ((dest >> 6) * 171) >> 9
    owned = iota((n_pack, tok), 0) == owner
    before = onehot(iota((tok, tok), 0) < iota((tok, tok), 1))
    counted = jnp.dot(onehot(owned), before, preferred_element_type=F32)
    slot = jnp.sum(jnp.where(owned, counted, 0.0), axis=0, keepdims=True).astype(jnp.int32)
    return owner, slot


def total_of(parts):
    return functools.reduce(lambda a, b: a + b, parts)


def pack_kernel(n_pack, chunks, first, labelled, dest_ref, rows_ref, out_ref):
    tok = rows_ref.shape[0]
    dest = dest_ref[...]
    owner, slot = slots_of(dest, n_pack, tok)
    row = iota((n_pack * 16, tok), 0)
    parts = {}
    for shift, pairs in tile_shifts(chunks).items():
        at = slot - shift
        key = jnp.where((at >= 0) & (at < 16), owner * 16 + at, -1)
        picked = jnp.concatenate(
            [rows_ref[:, (first + f) * LANES : (first + f + 1) * LANES] for _, f in pairs], axis=1
        )
        moved = jnp.dot(onehot(row == key), picked, preferred_element_type=F32)
        for n, (tile, _) in enumerate(pairs):
            parts.setdefault(tile, []).append(moved[:, n * LANES : (n + 1) * LANES])
    if labelled:
        place = dest - owner * tok
        tags = jnp.where(iota((LANES, tok), 0) == slot, (place + 1).astype(F32), 0.0).astype(BF)
        here = onehot(row == owner * 16 + CAP * chunks % 16)
        parts[max(parts)].append(lax.dot_general(here, tags, NT, preferred_element_type=F32))
    for tile in parts:
        block = total_of(parts[tile]).astype(BF)
        out_ref[:, tile * 16 : (tile + 1) * 16, :] = block.reshape(n_pack, 16, LANES)


def place_rows(n_pack, chunks, labels, in_ref, out_ref):
    tok = TOK
    group = n_pack * 16
    col = iota((n_pack, group), 1)
    lead = iota((n_pack, group), 0) * 16
    mine = (col >= lead) & (col < lead + 16)
    offset = iota((LANES, group), 0) - (iota((LANES, group), 1) & 15)
    place = iota((tok, group), 0) + 1
    parts = {}
    for shift, pairs in tile_shifts(chunks).items():
        spread = jnp.dot(labels, onehot(offset == shift), preferred_element_type=F32)
        label = jnp.sum(jnp.where(mine, spread, 0.0), axis=0, keepdims=True).astype(jnp.int32)
        picked = jnp.concatenate(
            [in_ref[:, t * 16 : (t + 1) * 16, :].reshape(group, LANES) for t, _ in pairs], axis=1
        )
        moved = jnp.dot(onehot(place == label), picked, preferred_element_type=F32)
        for n, (_, f) in enumerate(pairs):
            parts.setdefault(f, []).append(moved[:, n * LANES : (n + 1) * LANES])
    for f in parts:
        out_ref[0:tok, f * LANES : (f + 1) * LANES] = total_of(parts[f]).astype(BF)


def unpack_near_kernel(n_pack, in_ref, w_ref, out_ref, label_ref):
    group = n_pack * 16
    tile = in_ref[:, NEAR * CAP // 16 * 16 :, :].reshape(group, LANES)
    at = iota((n_pack, group), 0) * 16 + NEAR * CAP % 16
    labels = jnp.dot(
        onehot(iota((n_pack, group), 1) == at), tile, preferred_element_type=F32
    ).astype(BF)
    label_ref[...] = labels
    place_rows(n_pack, NEAR, labels, in_ref, out_ref)
    cut = NEAR * LANES
    rest = FAR * LANES
    out_ref[TOK : TOK + 64, :] = w_ref[0:64, 0:cut]
    out_ref[TOK + 64 : TOK + 128, 0:rest] = w_ref[0:64, cut:]
    out_ref[TOK + 64 : TOK + 128, rest:] = jnp.zeros((64, cut - rest), BF)
    last = w_ref[64:HD, :].astype(F32)
    low = last[:, 0:cut]
    high = jnp.concatenate([last[:, cut:], jnp.zeros((HD - 64, cut - rest), F32)], axis=1)
    out_ref[TOK + 128 : TOK + 160, :] = jnp.concatenate([low, low, high, high], axis=0).astype(BF)


def unpack_far_kernel(n_pack, in_ref, label_ref, out_ref):
    place_rows(n_pack, FAR, label_ref[...], in_ref, out_ref)


QT = 256
KT = 512
AROWS = 112
NEG = -3e38
LIMIT = pltpu.CompilerParams(vmem_limit_bytes=56 * 2**20)


def attend_kernel(
    steps, n_seq, order_ref, doc_ref, near_ref, mine_ref, pair_ref, w_ref, out_ref, q_s, k_s, v_s, o_s, bound_s
):
    step = pl.program_id(0)
    rows = pl.ds(pl.multiple_of(order_ref[step] * TOK, 64), TOK)
    far = jnp.where(step < steps // 2, mine_ref[0], pair_ref[0])
    x = jnp.concatenate([near_ref[0], far], axis=1)
    qkv = [
        lax.dot_general(x, w_ref[j], NT, preferred_element_type=F32).astype(BF) for j in range(3)
    ]
    q_s[rows, :] = qkv[0]
    k_s[rows, :] = qkv[1]
    v_s[rows, 0:HD] = qkv[2]
    v_s[rows, HD:LANES] = jnp.where(iota((TOK, LANES - HD), 1) == 0, 1.0, 0.0).astype(BF)

    @pl.when(step == steps - 1)
    def _():
        length = k_s.shape[0] - KT
        blocks = length // BLK
        scale = math.log2(math.e) / math.sqrt(HD)
        k_s[length:, :] = jnp.zeros((KT, HD), BF)
        v_s[length:, :] = jnp.zeros((KT, LANES), BF)
        first = jnp.int32(0)
        for b in range(blocks):
            if b:
                first = jnp.where(doc_ref[0, b * BLK] == doc_ref[0, (b - 1) * BLK], first, b)
            bound_s[0, b] = first
        last = jnp.int32(blocks)
        for b in reversed(range(blocks)):
            if b < blocks - 1:
                last = jnp.where(doc_ref[0, b * BLK] == doc_ref[0, (b + 1) * BLK], last, b + 1)
            bound_s[1, b] = last
        per = QT // BLK

        def one_tile(t, _):
            q = q_s[pl.ds(pl.multiple_of(t * QT, QT), QT), :]
            lo = bound_s[0, t * per]
            hi = bound_s[1, t * per + per - 1]
            chunks = (hi - lo + KT // BLK - 1) // (KT // BLK)

            def one_chunk(c, carry):
                high, total = carry
                begin = lo + c * (KT // BLK)
                keys = pl.ds(pl.multiple_of(begin * BLK, BLK), KT)
                scores = lax.dot_general(q, k_s[keys, :], NT, preferred_element_type=F32)
                block = begin + iota((1, KT), 1) // BLK
                halves = []
                for i in range(per):
                    keep = (block >= bound_s[0, t * per + i]) & (block < bound_s[1, t * per + i])
                    halves.append(
                        jnp.where(keep, scores[i * BLK : (i + 1) * BLK, :], -jnp.inf)
                    )
                scores = jnp.concatenate(halves, axis=0)
                newer = jnp.maximum(high, jnp.max(scores, axis=1, keepdims=True))
                expo = jnp.exp2((scores - newer) * scale).astype(BF)
                total = total * jnp.exp2((high - newer) * scale) + jnp.dot(
                    expo, v_s[keys, :], preferred_element_type=F32
                )
                return newer, total

            high = jnp.full((QT, 1), NEG, F32)
            total = jnp.zeros((QT, LANES), F32)
            _, total = lax.fori_loop(0, chunks, one_chunk, (high, total))
            done = total[:, 0:HD] / total[:, HD : HD + 1]
            o_s[pl.ds(pl.multiple_of(t * QT, QT), QT), 0:HD] = done
            return 0

        lax.fori_loop(0, length // QT, one_tile, 0)
        tok = length // n_seq
        for s in range(n_seq):
            turned = o_s[s * tok : (s + 1) * tok, :].T
            out_ref[s, 0:64, :] = turned[0:64, 0:LANES].astype(BF)
            out_ref[s, 64:96, :] = jnp.concatenate(
                [turned[0:32, LANES:tok], turned[32:64, LANES:tok]], axis=1
            ).astype(BF)
            out_ref[s, 96:112, :] = jnp.concatenate(
                [
                    turned[64:72, 0:LANES],
                    jnp.concatenate(
                        [turned[64:72, LANES:tok], jnp.zeros((8, 2 * LANES - tok), F32)], axis=1
                    ),
                ],
                axis=0,
            ).astype(BF)


def project_kernel(n_seq, in_ref, wa_ref, wb_ref, wc_ref, wd_ref, we_ref, out_ref):
    width = out_ref.shape[1]
    tok = out_ref.shape[0]
    rest = tok - LANES
    lo = in_ref[:, 0:32, :].reshape(n_seq * 32, LANES)
    hi = in_ref[:, 32:64, :].reshape(n_seq * 32, LANES)
    far = in_ref[:, 64:96, :].reshape(n_seq * 32, LANES)
    tail = in_ref[:, 96:112, :].reshape(n_seq * 16, LANES).astype(F32)
    upper = (iota(tail.shape, 0) & 15) < 8
    tail_near = jnp.where(upper, tail, 0.0).astype(BF)
    tail_far = jnp.where(upper, 0.0, tail).astype(BF)
    near = jnp.concatenate([lo, hi, tail_near], axis=0).T
    far_t = far.T
    distant = jnp.concatenate([far_t[0:rest], far_t[rest:LANES], tail_far.T[0:rest]], axis=1)
    left = jnp.concatenate([near, distant], axis=0)
    cut = NEAR * LANES
    for lo_ref, hi_ref, t, begin, end in (
        (wa_ref, wb_ref, 0, 0, cut),
        (wc_ref, wd_ref, 16, cut, width),
    ):
        weights = jnp.concatenate(
            [
                lo_ref[:, :, 0 : end - begin].reshape(n_seq * 32, end - begin),
                hi_ref[:, :, 0 : end - begin].reshape(n_seq * 32, end - begin),
                we_ref[:, t : t + 16, 0 : end - begin].reshape(n_seq * 16, end - begin),
            ],
            axis=0,
        )
        out_ref[:, begin:end] = jnp.dot(left, weights, preferred_element_type=F32).astype(BF)


def whole(*shape):
    return pl.BlockSpec(shape, lambda *_: (0,) * len(shape))


def attend_call(order, doc_ids, near, mine, pair, w_t):
    n_seq = near.shape[0]
    length = n_seq * TOK
    half = n_seq // 2
    far = (1, TOK, FAR * LANES)
    return pl.pallas_call(
        functools.partial(attend_kernel, n_seq, n_seq),
        grid_spec=pltpu.PrefetchScalarGridSpec(
            num_scalar_prefetch=1,
            grid=(n_seq,),
            in_specs=[
                pl.BlockSpec(memory_space=pltpu.SMEM),
                pl.BlockSpec((1, TOK, NEAR * LANES), lambda i, o: (o[i], 0, 0)),
                pl.BlockSpec(far, lambda i, o: (jnp.minimum(i, half - 1), 0, 0)),
                pl.BlockSpec(far, lambda i, o: (jnp.maximum(i - half, 0), 0, 0)),
                whole(*w_t.shape),
            ],
            out_specs=whole(n_seq, AROWS, LANES),
            scratch_shapes=[
                pltpu.VMEM((length, HD), BF),
                pltpu.VMEM((length + KT, HD), BF),
                pltpu.VMEM((length + KT, LANES), BF),
                pltpu.VMEM((length, LANES), F32),
                pltpu.SMEM((2, length // BLK), jnp.int32),
            ],
        ),
        out_shape=jax.ShapeDtypeStruct((n_seq, AROWS, LANES), BF),
        compiler_params=LIMIT,
        name="attend",
    )(order, doc_ids, near, mine, pair, w_t)


def ring_gather(block, n_seq):
    chips = n_seq // 2
    up = [(i, (i + 2) % n_seq) for i in range(n_seq)]
    down = [(i, (i - 2) % n_seq) for i in range(n_seq)]
    right = left = block
    held = [block]
    for _ in range((chips - 1) // 2):
        right = lax.ppermute(right, "seq", up)
        left = lax.ppermute(left, "seq", down)
        held += [right, left]
    middle = block.shape[0] // 2
    held += [
        lax.ppermute(right[:middle], "seq", up),
        lax.ppermute(left[middle:], "seq", down),
    ]
    return jnp.concatenate(held, axis=0).reshape(chips, *block.shape)


def local_call(kernel, out_shape, *operands, name):
    return pl.pallas_call(kernel, out_shape=out_shape, compiler_params=LIMIT, name=name)(*operands)


def body(source, destination, doc_ids, w_qkv, w_out):
    n_pack = lax.axis_size("pack")
    n_seq = lax.axis_size("seq")
    width = source.shape[2]
    shape = jax.ShapeDtypeStruct
    near_rows = NEAR * CAP // 16 * 16 + 16
    far_rows = FAR * CAP

    def exchange(outbox):
        return lax.all_to_all(outbox, "pack", split_axis=0, concat_axis=0, tiled=True)

    def packed_rows(chunks, first, labelled, rows, name):
        return local_call(
            functools.partial(pack_kernel, n_pack, chunks, first, labelled),
            shape((n_pack, rows, LANES), BF),
            destination,
            source[0],
            name=name,
        )

    near_box = exchange(packed_rows(NEAR, 0, True, near_rows, "pack_near"))
    far_out = packed_rows(FAR, NEAR, False, far_rows, "pack_far")
    near_box, far_out = lax.optimization_barrier((near_box, far_out))
    far_box = exchange(far_out)
    near, labels = local_call(
        functools.partial(unpack_near_kernel, n_pack),
        (shape((TOK + 160, NEAR * LANES), BF), shape((n_pack, LANES), BF)),
        near_box,
        w_out,
        name="unpack_near",
    )
    near_all = lax.all_gather(near, "seq", axis=0, tiled=False)
    far = local_call(
        functools.partial(unpack_far_kernel, n_pack),
        shape((TOK, FAR * LANES), BF),
        far_box,
        labels,
        name="unpack_far",
    )
    mine = ring_gather(far, n_seq)
    pair = lax.ppermute(mine, "seq", [(i, i ^ 1) for i in range(n_seq)])

    me = lax.axis_index("seq").astype(jnp.int32)
    back = jnp.array([0, 1, -1, 2, -2, 3, -3, 4], jnp.int32)
    chip = lax.rem(me // 2 - back + n_seq // 2, n_seq // 2)
    core = me % 2
    order = jnp.concatenate([2 * chip + core, 2 * chip + 1 - core])
    attended = attend_call(
        order, doc_ids, near_all, mine, pair, jnp.transpose(w_qkv, (0, 2, 1))
    )
    blocks = lax.all_to_all(attended, "seq", split_axis=0, concat_axis=0, tiled=True)

    def w_spec(n):
        return pl.BlockSpec((n_seq, 32, NEAR * LANES), lambda i: (0, TOK // 32 + n, 0))

    out = pl.pallas_call(
        functools.partial(project_kernel, n_seq),
        grid=(1,),
        out_shape=shape((TOK, width), BF),
        in_specs=[whole(*blocks.shape)] + [w_spec(n) for n in range(5)],
        out_specs=whole(TOK, width),
        compiler_params=LIMIT,
        name="project",
    )(blocks, near_all, near_all, near_all, near_all, near_all)
    return out[None]


def solution(mesh):
    placed = (
        P("seq", "pack", None),
        P("seq", "pack"),
        P("pack", None),
        P(None, None, "seq"),
        P("seq", None),
    )
    return jax.shard_map(
        body, mesh=mesh, in_specs=placed, out_specs=P("pack", "seq", None), check_vma=False
    )
```

```python
import functools
import math

import jax
import jax.numpy as jnp
from jax import lax
from jax.experimental import pallas as pl
from jax.experimental.pallas import tpu as pltpu
from jax.sharding import PartitionSpec as P

HD = 72
CAP = 12
LANES = 128
BLK = 128
BF = jnp.bfloat16
F32 = jnp.float32
NT = (((1,), (1,)), ((), ()))

SHIFTS = (
    (0, ((0, 0), (3, 4), (6, 8))),
    (-12, ((0, 1), (3, 5))),
    (4, ((1, 1), (4, 5))),
    (-8, ((1, 2), (4, 6))),
    (8, ((2, 2), (5, 6))),
    (-4, ((2, 3), (5, 7))),
)
TILES = 7


def iota(shape, dim):
    return lax.broadcasted_iota(jnp.int32, shape, dim)


def onehot(condition):
    return jnp.where(condition, 1.0, 0.0).astype(BF)


def pack_kernel(n_pack, dest_ref, rows_ref, out_ref):
    tok = rows_ref.shape[0]
    group = n_pack * 16
    dest = dest_ref[...]
    owner = ((dest >> 6) * 171) >> 9
    place = dest - owner * tok
    owned = iota((n_pack, tok), 0) == owner
    before = onehot(iota((tok, tok), 0) < iota((tok, tok), 1))
    counted = jnp.dot(onehot(owned), before, preferred_element_type=F32)
    slot = jnp.sum(jnp.where(owned, counted, 0.0), axis=0, keepdims=True).astype(jnp.int32)
    row = iota((group, tok), 0)
    parts = {}
    for shift, pairs in SHIFTS:
        at = slot - shift
        key = jnp.where((at >= 0) & (at < 16), owner * 16 + at, -1)
        picked = jnp.concatenate(
            [rows_ref[:, f * LANES : (f + 1) * LANES] for _, f in pairs], axis=1
        )
        moved = jnp.dot(onehot(row == key), picked, preferred_element_type=F32)
        for n, (tile, _) in enumerate(pairs):
            parts.setdefault(tile, []).append(moved[:, n * LANES : (n + 1) * LANES])
    tags = jnp.where(iota((LANES, tok), 0) == slot, (place + 1).astype(F32), 0.0).astype(BF)
    here = onehot(row == owner * 16 + CAP)
    parts[TILES - 1].append(lax.dot_general(here, tags, NT, preferred_element_type=F32))
    for tile in range(TILES):
        whole = functools.reduce(lambda a, b: a + b, parts[tile])
        out_ref[:, tile * 16 : (tile + 1) * 16, :] = whole.astype(BF).reshape(n_pack, 16, LANES)


def unpack_kernel(n_pack, in_ref, out_ref):
    tok = out_ref.shape[0]
    group = n_pack * 16
    tiles = [in_ref[:, t * 16 : (t + 1) * 16, :].reshape(group, LANES) for t in range(TILES)]
    col = iota((n_pack, group), 1)
    lead = iota((n_pack, group), 0) * 16
    labels = jnp.dot(onehot(col == lead + CAP), tiles[-1], preferred_element_type=F32).astype(BF)
    mine = (col >= lead) & (col < lead + 16)
    offset = iota((LANES, group), 0) - (iota((LANES, group), 1) & 15)
    place = iota((tok, group), 0) + 1
    parts = {}
    for shift, pairs in SHIFTS:
        spread = jnp.dot(labels, onehot(offset == shift), preferred_element_type=F32)
        label = jnp.sum(jnp.where(mine, spread, 0.0), axis=0, keepdims=True).astype(jnp.int32)
        picked = jnp.concatenate([tiles[t] for t, _ in pairs], axis=1)
        moved = jnp.dot(onehot(place == label), picked, preferred_element_type=F32)
        for n, (_, f) in enumerate(pairs):
            parts.setdefault(f, []).append(moved[:, n * LANES : (n + 1) * LANES])
    for f in sorted(parts):
        whole = functools.reduce(lambda a, b: a + b, parts[f])
        out_ref[:, f * LANES : (f + 1) * LANES] = whole.astype(BF)


TOKT = 1024
QT = 256
KT = 1024
SIDE = 1
VROWS = 80
AROWS = 112
NEG = -3e38
LIMIT = pltpu.CompilerParams(vmem_limit_bytes=56 * 2**20)


def attend_kernel(steps, n_seq, doc_ref, x_ref, w_ref, out_ref, q_s, k_s, v_s, o_s, bound_s):
    step = pl.program_id(0)
    start = pl.multiple_of(step * TOKT, TOKT)
    qkv = lax.dot_general(x_ref[...], w_ref[...], NT, preferred_element_type=F32)
    q_s[pl.ds(start, TOKT), :] = (qkv[:, 0:HD] * (1.0 / math.sqrt(HD))).astype(BF)
    k_s[pl.ds(start, TOKT), :] = qkv[:, HD : 2 * HD].astype(BF)
    turned = qkv[:, LANES : 3 * HD].T[2 * HD - LANES :, :]
    ones = jnp.ones((VROWS - HD, TOKT), F32)
    v_s[:, pl.ds(start, TOKT)] = jnp.concatenate([turned, ones], axis=0).astype(BF)

    @pl.when(step == steps - 1)
    def _():
        length = q_s.shape[0]
        blocks = length // BLK
        per_q = QT // BLK
        per_k = KT // BLK
        k_s[length:, :] = jnp.zeros((KT, HD), BF)
        v_s[:, length:] = jnp.zeros((VROWS, KT), BF)
        first = jnp.int32(0)
        for b in range(blocks):
            if b:
                first = jnp.where(doc_ref[0, b * BLK] == doc_ref[0, (b - 1) * BLK], first, b)
            bound_s[0, b] = first
        last = jnp.int32(blocks)
        for b in reversed(range(blocks)):
            if b < blocks - 1:
                last = jnp.where(doc_ref[0, b * BLK] == doc_ref[0, (b + 1) * BLK], last, b + 1)
            bound_s[1, b] = last

        def some_tiles(group, _):
            tiles = []
            for u in range(SIDE):
                t = group * SIDE + u
                bounds = [
                    (bound_s[0, t * per_q + i], bound_s[1, t * per_q + i]) for i in range(per_q)
                ]
                q = q_s[pl.ds(pl.multiple_of(t * QT, QT), QT), :]
                tiles.append((t, q, bounds))
            chunks = functools.reduce(
                jnp.maximum, [b[-1][1] - b[0][0] for _, _, b in tiles]
            )
            chunks = (chunks + per_k - 1) // per_k

            def one_chunk(c, carry):
                result = []
                for (_, q, bounds), (high, total) in zip(tiles, carry):
                    begin = bounds[0][0] + c * per_k
                    keys = pl.ds(pl.multiple_of(jnp.minimum(begin, blocks) * BLK, BLK), KT)
                    scores = lax.dot_general(k_s[keys, :], q, NT, preferred_element_type=F32)
                    columns = []
                    for i, (lo, hi) in enumerate(bounds):
                        kept = [
                            jnp.where(
                                (begin + j >= lo) & (begin + j < hi),
                                scores[j * BLK : (j + 1) * BLK, i * BLK : (i + 1) * BLK],
                                -jnp.inf,
                            )
                            for j in range(per_k)
                        ]
                        columns.append(jnp.concatenate(kept, axis=0))
                    scores = jnp.concatenate(columns, axis=1)
                    newer = jnp.maximum(high, jnp.max(scores, axis=0, keepdims=True))
                    expo = jnp.exp(scores - newer).astype(BF)
                    total = total * jnp.exp(high - newer) + jnp.dot(
                        v_s[:, keys], expo, preferred_element_type=F32
                    )
                    result.append((newer, total))
                return tuple(result)

            carry = tuple(
                (jnp.full((1, QT), NEG, F32), jnp.zeros((VROWS, QT), F32)) for _ in range(SIDE)
            )
            for (t, _, _), (_, total) in zip(tiles, lax.fori_loop(0, chunks, one_chunk, carry)):
                o_s[:, pl.ds(pl.multiple_of(t * QT, QT), QT)] = total / total[HD : HD + 1, :]
            return 0

        lax.fori_loop(0, length // (QT * SIDE), some_tiles, 0)
        tok = length // n_seq
        for s in range(n_seq):
            mine = o_s[0:HD, s * tok : (s + 1) * tok]
            rest = mine[:, LANES:tok]
            out_ref[s, 0:64, :] = mine[0:64, 0:LANES].astype(BF)
            out_ref[s, 64:96, :] = jnp.concatenate([rest[0:32], rest[32:64]], axis=1).astype(BF)
            empty = jnp.zeros((HD - 64, 2 * LANES - tok), F32)
            out_ref[s, 96:112, :] = jnp.concatenate(
                [mine[64:HD, 0:LANES], jnp.concatenate([rest[64:HD], empty], axis=1)], axis=0
            ).astype(BF)


def project_kernel(n_seq, in_ref, w_ref, out_ref):
    width = out_ref.shape[1]
    tok = out_ref.shape[0]
    rest = tok - LANES
    lo = in_ref[:, 0:32, :].reshape(n_seq * 32, LANES)
    hi = in_ref[:, 32:64, :].reshape(n_seq * 32, LANES)
    far = in_ref[:, 64:96, :].reshape(n_seq * 32, LANES)
    tail = in_ref[:, 96:112, :].reshape(n_seq * 16, LANES).astype(F32)
    upper = (iota(tail.shape, 0) & 15) < 8
    tail_near = jnp.where(upper, tail, 0.0).astype(BF)
    tail_far = jnp.where(upper, 0.0, tail).astype(BF)
    near = jnp.concatenate([lo, hi, tail_near], axis=0).T
    far_t = far.T
    distant = jnp.concatenate([far_t[0:rest], far_t[rest:LANES], tail_far.T[0:rest]], axis=1)
    left = jnp.concatenate([near, distant], axis=0)
    last = w_ref[:, 64:HD, :].astype(F32)
    weights = jnp.concatenate(
        [
            w_ref[:, 0:32, :].reshape(n_seq * 32, width),
            w_ref[:, 32:64, :].reshape(n_seq * 32, width),
            jnp.concatenate([last, last], axis=1).reshape(n_seq * 16, width).astype(BF),
        ],
        axis=0,
    )
    out_ref[...] = jnp.dot(left, weights, preferred_element_type=F32).astype(BF)


def whole(*shape):
    return pl.BlockSpec(shape, lambda *_: (0,) * len(shape))


def attend_call(doc_ids, tokens, w_t, n_seq):
    length, width = tokens.shape
    steps = length // TOKT
    return pl.pallas_call(
        functools.partial(attend_kernel, steps, n_seq),
        grid=(steps,),
        out_shape=jax.ShapeDtypeStruct((n_seq, AROWS, LANES), BF),
        in_specs=[
            pl.BlockSpec(memory_space=pltpu.SMEM),
            pl.BlockSpec((TOKT, width), lambda i: (i, 0)),
            whole(*w_t.shape),
        ],
        out_specs=whole(n_seq, AROWS, LANES),
        scratch_shapes=[
            pltpu.VMEM((length, HD), BF),
            pltpu.VMEM((length + KT, HD), BF),
            pltpu.VMEM((VROWS, length + KT), BF),
            pltpu.VMEM((VROWS, length), F32),
            pltpu.SMEM((2, length // BLK), jnp.int32),
        ],
        compiler_params=LIMIT,
        name="attend",
    )(doc_ids, tokens, w_t)


def body(source, destination, doc_ids, w_qkv, w_out):
    n_pack = lax.axis_size("pack")
    n_seq = lax.axis_size("seq")
    tok, width = source.shape[1:]
    w_all = lax.all_gather(w_out, "seq", axis=0, tiled=False)

    outbox = pl.pallas_call(
        functools.partial(pack_kernel, n_pack),
        out_shape=jax.ShapeDtypeStruct((n_pack, TILES * 16, LANES), BF),
        compiler_params=LIMIT,
        name="pack_rows",
    )(destination, source[0])
    inbox = lax.all_to_all(outbox, "pack", split_axis=0, concat_axis=0, tiled=True)
    packed = pl.pallas_call(
        functools.partial(unpack_kernel, n_pack),
        out_shape=jax.ShapeDtypeStruct((tok, width), BF),
        compiler_params=LIMIT,
        name="unpack_rows",
    )(inbox)
    packed, w_all = lax.optimization_barrier((packed, w_all))
    tokens = lax.all_gather(packed, "seq", axis=0, tiled=True)

    attended = attend_call(
        doc_ids, tokens, jnp.transpose(w_qkv, (0, 2, 1)).reshape(3 * HD, width), n_seq
    )
    blocks = lax.all_to_all(attended, "seq", split_axis=0, concat_axis=0, tiled=True)

    out = pl.pallas_call(
        functools.partial(project_kernel, n_seq),
        out_shape=jax.ShapeDtypeStruct((tok, width), BF),
        compiler_params=LIMIT,
        name="project",
    )(blocks, w_all)
    return out[None]


def solution(mesh):
    placed = (
        P("seq", "pack", None),
        P("seq", "pack"),
        P("pack", None),
        P(None, None, "seq"),
        P("seq", None),
    )
    return jax.shard_map(
        body, mesh=mesh, in_specs=placed, out_specs=P("pack", "seq", None), check_vma=False
    )
```

```python
import functools
import math

import jax
import jax.numpy as jnp
from jax import lax
from jax.experimental import pallas as pl
from jax.experimental.pallas import tpu as pltpu
from jax.sharding import PartitionSpec as P

HD = 72
CAP = 12
LANES = 128
BLK = 128
BF = jnp.bfloat16
F32 = jnp.float32
NT = (((1,), (1,)), ((), ()))

SHIFTS = (
    (0, ((0, 0), (3, 4), (6, 8))),
    (-12, ((0, 1), (3, 5))),
    (4, ((1, 1), (4, 5))),
    (-8, ((1, 2), (4, 6))),
    (8, ((2, 2), (5, 6))),
    (-4, ((2, 3), (5, 7))),
)
TILES = 7


def iota(shape, dim):
    return lax.broadcasted_iota(jnp.int32, shape, dim)


def onehot(condition):
    return jnp.where(condition, 1.0, 0.0).astype(BF)


def pack_kernel(n_pack, dest_ref, rows_ref, out_ref):
    tok = rows_ref.shape[0]
    group = n_pack * 16
    dest = dest_ref[...]
    owner = ((dest >> 6) * 171) >> 9
    place = dest - owner * tok
    owned = iota((n_pack, tok), 0) == owner
    before = onehot(iota((tok, tok), 0) < iota((tok, tok), 1))
    counted = jnp.dot(onehot(owned), before, preferred_element_type=F32)
    slot = jnp.sum(jnp.where(owned, counted, 0.0), axis=0, keepdims=True).astype(jnp.int32)
    row = iota((group, tok), 0)
    parts = {}
    for shift, pairs in SHIFTS:
        at = slot - shift
        key = jnp.where((at >= 0) & (at < 16), owner * 16 + at, -1)
        picked = jnp.concatenate(
            [rows_ref[:, f * LANES : (f + 1) * LANES] for _, f in pairs], axis=1
        )
        moved = jnp.dot(onehot(row == key), picked, preferred_element_type=F32)
        for n, (tile, _) in enumerate(pairs):
            parts.setdefault(tile, []).append(moved[:, n * LANES : (n + 1) * LANES])
    tags = jnp.where(iota((LANES, tok), 0) == slot, (place + 1).astype(F32), 0.0).astype(BF)
    here = onehot(row == owner * 16 + CAP)
    parts[TILES - 1].append(lax.dot_general(here, tags, NT, preferred_element_type=F32))
    for tile in range(TILES):
        whole = functools.reduce(lambda a, b: a + b, parts[tile])
        out_ref[:, tile * 16 : (tile + 1) * 16, :] = whole.astype(BF).reshape(n_pack, 16, LANES)


def unpack_kernel(n_pack, in_ref, *refs):
    out_ref = refs[-1]
    tok = out_ref.shape[0]
    group = n_pack * 16
    tiles = [in_ref[:, t * 16 : (t + 1) * 16, :].reshape(group, LANES) for t in range(TILES)]
    col = iota((n_pack, group), 1)
    lead = iota((n_pack, group), 0) * 16
    labels = jnp.dot(onehot(col == lead + CAP), tiles[-1], preferred_element_type=F32).astype(BF)
    mine = (col >= lead) & (col < lead + 16)
    offset = iota((LANES, group), 0) - (iota((LANES, group), 1) & 15)
    place = iota((tok, group), 0) + 1
    parts = {}
    for shift, pairs in SHIFTS:
        spread = jnp.dot(labels, onehot(offset == shift), preferred_element_type=F32)
        label = jnp.sum(jnp.where(mine, spread, 0.0), axis=0, keepdims=True).astype(jnp.int32)
        picked = jnp.concatenate([tiles[t] for t, _ in pairs], axis=1)
        moved = jnp.dot(onehot(place == label), picked, preferred_element_type=F32)
        for n, (_, f) in enumerate(pairs):
            parts.setdefault(f, []).append(moved[:, n * LANES : (n + 1) * LANES])
    for f in sorted(parts):
        whole = functools.reduce(lambda a, b: a + b, parts[f])
        out_ref[:, f * LANES : (f + 1) * LANES] = whole.astype(BF)


TOK = 192
QT = 256
KT = 1024
SIDE = 1
VROWS = 80
QKV = 256
AROWS = 112
NEG = -3e38
BACK = (0, 1, -1, 2, -2, 3, -3, 4)
LIMIT = pltpu.CompilerParams(vmem_limit_bytes=56 * 2**20)


def origin(me, n):
    chips = len(BACK)
    core = me & 1
    chip = ((me >> 1) - BACK[n % chips]) & (chips - 1)
    return 2 * chip + (core if n < chips else 1 - core)


def qkv_kernel(*refs):
    *x_refs, mine_w_ref, pair_w_ref, mine_ref, pair_ref = refs
    x = jnp.concatenate([ref[...] for ref in x_refs], axis=0)
    rows = x.shape[0]
    scale = jnp.where(iota((1, 3 * HD), 1) < HD, 1.0 / math.sqrt(HD), 1.0)
    fill = jnp.where(iota((rows, QKV - 3 * HD), 1) < VROWS - HD, 1.0, 0.0)
    for w_ref, out_ref in ((mine_w_ref, mine_ref), (pair_w_ref, pair_ref)):
        qkv = lax.dot_general(x, w_ref[...], NT, preferred_element_type=F32) * scale
        whole = jnp.concatenate([qkv, fill], axis=1).astype(BF)
        out_ref[...] = whole.reshape(rows // TOK, TOK, QKV)


def attend_kernel(n_seq, me_ref, doc_ref, *refs):
    *in_refs, out_ref, q_s, k_s, row_s, v_s, o_s, bound_s = refs
    n = 0
    for ref in in_refs:
        for i in range(ref.shape[0]):
            rows = pl.ds(pl.multiple_of(origin(me_ref[0], n) * TOK, 64), TOK)
            q_s[rows, :] = ref[i, :, 0:HD]
            k_s[rows, :] = ref[i, :, HD : 2 * HD]
            row_s[rows, :] = ref[i, :, LANES:QKV]
            n += 1
    length = q_s.shape[0]
    blocks = length // BLK
    per_q = QT // BLK
    per_k = KT // BLK
    for b in range(blocks):
        turned = row_s[b * BLK : (b + 1) * BLK, :].T
        begin = 2 * HD - LANES
        v_s[:, b * BLK : (b + 1) * BLK] = turned[begin : begin + VROWS, :]
    k_s[length:, :] = jnp.zeros((KT, HD), BF)
    v_s[:, length:] = jnp.zeros((VROWS, KT), BF)
    first = jnp.int32(0)
    for b in range(blocks):
        if b:
            first = jnp.where(doc_ref[0, b * BLK] == doc_ref[0, (b - 1) * BLK], first, b)
        bound_s[0, b] = first
    last = jnp.int32(blocks)
    for b in reversed(range(blocks)):
        if b < blocks - 1:
            last = jnp.where(doc_ref[0, b * BLK] == doc_ref[0, (b + 1) * BLK], last, b + 1)
        bound_s[1, b] = last

    def some_tiles(group, _):
        tiles = []
        for u in range(SIDE):
            t = group * SIDE + u
            bounds = [
                (bound_s[0, t * per_q + i], bound_s[1, t * per_q + i]) for i in range(per_q)
            ]
            q = q_s[pl.ds(pl.multiple_of(t * QT, QT), QT), :]
            tiles.append((t, q, bounds))
        chunks = functools.reduce(
            jnp.maximum, [b[-1][1] - b[0][0] for _, _, b in tiles]
        )
        chunks = (chunks + per_k - 1) // per_k

        def one_chunk(c, carry):
            result = []
            for (_, q, bounds), (high, total) in zip(tiles, carry):
                begin = bounds[0][0] + c * per_k
                keys = pl.ds(pl.multiple_of(jnp.minimum(begin, blocks) * BLK, BLK), KT)
                scores = lax.dot_general(k_s[keys, :], q, NT, preferred_element_type=F32)
                columns = []
                for i, (lo, hi) in enumerate(bounds):
                    kept = [
                        jnp.where(
                            (begin + j >= lo) & (begin + j < hi),
                            scores[j * BLK : (j + 1) * BLK, i * BLK : (i + 1) * BLK],
                            -jnp.inf,
                        )
                        for j in range(per_k)
                    ]
                    columns.append(jnp.concatenate(kept, axis=0))
                scores = jnp.concatenate(columns, axis=1)
                newer = jnp.maximum(high, jnp.max(scores, axis=0, keepdims=True))
                expo = jnp.exp(scores - newer).astype(BF)
                total = total * jnp.exp(high - newer) + jnp.dot(
                    v_s[:, keys], expo, preferred_element_type=F32
                )
                result.append((newer, total))
            return tuple(result)

        carry = tuple(
            (jnp.full((1, QT), NEG, F32), jnp.zeros((VROWS, QT), F32)) for _ in range(SIDE)
        )
        for (t, _, _), (_, total) in zip(tiles, lax.fori_loop(0, chunks, one_chunk, carry)):
            o_s[:, pl.ds(pl.multiple_of(t * QT, QT), QT)] = total / total[HD : HD + 1, :]
        return 0

    lax.fori_loop(0, length // (QT * SIDE), some_tiles, 0)
    tok = length // n_seq
    for s in range(n_seq):
        mine = o_s[0:HD, s * tok : (s + 1) * tok]
        rest = mine[:, LANES:tok]
        out_ref[s, 0:64, :] = mine[0:64, 0:LANES].astype(BF)
        out_ref[s, 64:96, :] = jnp.concatenate([rest[0:32], rest[32:64]], axis=1).astype(BF)
        empty = jnp.zeros((HD - 64, 2 * LANES - tok), F32)
        out_ref[s, 96:112, :] = jnp.concatenate(
            [mine[64:HD, 0:LANES], jnp.concatenate([rest[64:HD], empty], axis=1)], axis=0
        ).astype(BF)


def project_kernel(n_seq, me_ref, in_ref, mine_w_ref, pair_w_ref, out_ref):
    width = out_ref.shape[1]
    tok = out_ref.shape[0]
    rest = tok - LANES
    half = n_seq // 2
    came = [origin(me_ref[0], n) for n in range(n_seq)]

    def features(begin, end):
        return jnp.concatenate([in_ref[s, begin:end, :] for s in came], axis=0)

    lo = features(0, 32)
    hi = features(32, 64)
    far = features(64, 96)
    tail = features(96, 112).astype(F32)
    upper = (iota(tail.shape, 0) & 15) < 8
    tail_near = jnp.where(upper, tail, 0.0).astype(BF)
    tail_far = jnp.where(upper, 0.0, tail).astype(BF)
    near = jnp.concatenate([lo, hi, tail_near], axis=0).T
    far_t = far.T
    distant = jnp.concatenate([far_t[0:rest], far_t[rest:LANES], tail_far.T[0:rest]], axis=1)
    left = jnp.concatenate([near, distant], axis=0)
    weights = []
    for begin in (0, 32):
        for ref in (mine_w_ref, pair_w_ref):
            weights.append(ref[:, begin : begin + 32, :].reshape(half * 32, width))
    for ref in (mine_w_ref, pair_w_ref):
        last = ref[:, 64:HD, :].astype(F32)
        weights.append(jnp.concatenate([last, last], axis=1).reshape(half * 16, width).astype(BF))
    weights = jnp.concatenate(weights, axis=0)
    out_ref[...] = jnp.dot(left, weights, preferred_element_type=F32).astype(BF)


def cost(flops, operands, out_shape):
    total = sum(math.prod(x.shape) * x.dtype.itemsize for x in operands)
    total += sum(math.prod(x.shape) * x.dtype.itemsize for x in jax.tree.leaves(out_shape))
    return pl.CostEstimate(flops=flops, bytes_accessed=total, transcendentals=0)


def local_call(kernel, out_shape, *operands, name, flops, small=0, scratch=(), behind=()):
    smem = pl.BlockSpec(memory_space=pltpu.SMEM)
    vmem = pl.BlockSpec(memory_space=pltpu.VMEM)
    after = [pl.BlockSpec(memory_space=pl.ANY)] * len(behind)
    return pl.pallas_call(
        kernel,
        out_shape=out_shape,
        in_specs=[smem] * small + [vmem] * (len(operands) - small) + after,
        out_specs=jax.tree.map(lambda _: vmem, out_shape),
        scratch_shapes=scratch,
        compiler_params=LIMIT,
        cost_estimate=cost(flops, operands, out_shape),
        name=name,
    )(*operands, *behind)


def project_qkv(blocks, mine_w, pair_w, name):
    rows = sum(x.shape[0] for x in blocks)
    out = jax.ShapeDtypeStruct((rows // TOK, TOK, QKV), BF)
    flops = 2 * rows * mine_w.shape[1] * 6 * HD
    return local_call(
        qkv_kernel, (out, out), *blocks, mine_w, pair_w, name=name, flops=flops
    )


def attend_call(me, doc_ids, n_seq, *blocks):
    length = n_seq * TOK
    return local_call(
        functools.partial(attend_kernel, n_seq),
        jax.ShapeDtypeStruct((n_seq, AROWS, LANES), BF),
        me,
        doc_ids,
        *blocks,
        small=2,
        flops=2 * length * length * HD,
        scratch=[
            pltpu.VMEM((length, HD), BF),
            pltpu.VMEM((length + KT, HD), BF),
            pltpu.VMEM((length, LANES), BF),
            pltpu.VMEM((VROWS, length + KT), BF),
            pltpu.VMEM((VROWS, length), F32),
            pltpu.SMEM((2, length // BLK), jnp.int32),
        ],
        name="attend",
    )


def ring_step(right, left, n_seq):
    up = [(i, (i + 2) % n_seq) for i in range(n_seq)]
    down = [(i, (i - 2) % n_seq) for i in range(n_seq)]
    return lax.ppermute(right, "seq", up), lax.ppermute(left, "seq", down)


def body(source, destination, doc_ids, w_qkv, w_out):
    n_pack = lax.axis_size("pack")
    n_seq = lax.axis_size("seq")
    width = source.shape[2]
    shape = jax.ShapeDtypeStruct
    me = lax.axis_index("seq").astype(jnp.int32).reshape(1)
    w_t = jnp.transpose(w_qkv, (0, 2, 1)).reshape(3 * HD, width)

    def other_core(x):
        return lax.ppermute(x, "seq", [(i, i ^ 1) for i in range(n_seq)])

    outbox = local_call(
        functools.partial(pack_kernel, n_pack),
        shape((n_pack, TILES * 16, LANES), BF),
        destination,
        source[0],
        name="pack_rows",
        flops=10**9,
    )
    inbox = lax.all_to_all(outbox, "pack", split_axis=0, concat_axis=0, tiled=True)

    pair_w = other_core(w_t)
    right = left = w_out
    held = [w_out]
    for _ in range(3):
        right, left = ring_step(right, left, n_seq)
        held += [right, left]
    held.append(ring_step(right, left, n_seq)[0])
    w_mine = jnp.stack(held)
    w_pair = other_core(w_mine)

    packed = local_call(
        functools.partial(unpack_kernel, n_pack),
        shape((TOK, width), BF),
        inbox,
        name="unpack_rows",
        flops=10**9,
        behind=(w_pair, pair_w),
    )
    right = left = packed
    held = [packed]
    for _ in range(3):
        right, left = ring_step(right, left, n_seq)
        held += [right, left]
    held += ring_step(right[: TOK // 2], left[TOK // 2 :], n_seq)

    mine_a, theirs_a = project_qkv(held[:5], w_t, pair_w, "qkv_first")
    mine_b, theirs_b = project_qkv(held[5:], w_t, pair_w, "qkv_last")
    attended = attend_call(
        me, doc_ids, n_seq, mine_a, mine_b, other_core(theirs_a), other_core(theirs_b)
    )
    blocks = lax.all_to_all(attended, "seq", split_axis=0, concat_axis=0, tiled=True)

    out = local_call(
        functools.partial(project_kernel, n_seq),
        shape((TOK, width), BF),
        me,
        blocks,
        w_mine,
        w_pair,
        name="project",
        flops=2 * TOK * width * width,
        small=1,
    )
    return out[None]


def solution(mesh):
    placed = (
        P("seq", "pack", None),
        P("seq", "pack"),
        P("pack", None),
        P(None, None, "seq"),
        P("seq", None),
    )
    return jax.shard_map(
        body, mesh=mesh, in_specs=placed, out_specs=P("pack", "seq", None), check_vma=False
    )
```

```python
import functools
import math

import jax
import jax.numpy as jnp
from jax import lax
from jax.experimental import pallas as pl
from jax.experimental.pallas import tpu as pltpu
from jax.sharding import PartitionSpec as P

HD = 72
CAP = 12
LANES = 128
BLK = 128
BF = jnp.bfloat16
F32 = jnp.float32
NT = (((1,), (1,)), ((), ()))

SHIFTS = (
    (0, ((0, 0), (3, 4), (6, 8))),
    (-12, ((0, 1), (3, 5))),
    (4, ((1, 1), (4, 5))),
    (-8, ((1, 2), (4, 6))),
    (8, ((2, 2), (5, 6))),
    (-4, ((2, 3), (5, 7))),
)
TILES = 7


def iota(shape, dim):
    return lax.broadcasted_iota(jnp.int32, shape, dim)


def onehot(condition):
    return jnp.where(condition, 1.0, 0.0).astype(BF)


def pack_kernel(n_pack, dest_ref, rows_ref, out_ref):
    tok = rows_ref.shape[0]
    group = n_pack * 16
    dest = dest_ref[...]
    owner = ((dest >> 6) * 171) >> 9
    place = dest - owner * tok
    owned = iota((n_pack, tok), 0) == owner
    before = onehot(iota((tok, tok), 0) < iota((tok, tok), 1))
    counted = jnp.dot(onehot(owned), before, preferred_element_type=F32)
    slot = jnp.sum(jnp.where(owned, counted, 0.0), axis=0, keepdims=True).astype(jnp.int32)
    row = iota((group, tok), 0)
    parts = {}
    for shift, pairs in SHIFTS:
        at = slot - shift
        key = jnp.where((at >= 0) & (at < 16), owner * 16 + at, -1)
        picked = jnp.concatenate(
            [rows_ref[:, f * LANES : (f + 1) * LANES] for _, f in pairs], axis=1
        )
        moved = jnp.dot(onehot(row == key), picked, preferred_element_type=F32)
        for n, (tile, _) in enumerate(pairs):
            parts.setdefault(tile, []).append(moved[:, n * LANES : (n + 1) * LANES])
    tags = jnp.where(iota((LANES, tok), 0) == slot, (place + 1).astype(F32), 0.0).astype(BF)
    here = onehot(row == owner * 16 + CAP)
    parts[TILES - 1].append(lax.dot_general(here, tags, NT, preferred_element_type=F32))
    for tile in range(TILES):
        whole = functools.reduce(lambda a, b: a + b, parts[tile])
        out_ref[:, tile * 16 : (tile + 1) * 16, :] = whole.astype(BF).reshape(n_pack, 16, LANES)


def unpack_kernel(n_pack, in_ref, w_ref, out_ref):
    tok = TOK
    group = n_pack * 16
    tiles = [in_ref[:, t * 16 : (t + 1) * 16, :].reshape(group, LANES) for t in range(TILES)]
    col = iota((n_pack, group), 1)
    lead = iota((n_pack, group), 0) * 16
    labels = jnp.dot(onehot(col == lead + CAP), tiles[-1], preferred_element_type=F32).astype(BF)
    mine = (col >= lead) & (col < lead + 16)
    offset = iota((LANES, group), 0) - (iota((LANES, group), 1) & 15)
    place = iota((tok, group), 0) + 1
    parts = {}
    for shift, pairs in SHIFTS:
        spread = jnp.dot(labels, onehot(offset == shift), preferred_element_type=F32)
        label = jnp.sum(jnp.where(mine, spread, 0.0), axis=0, keepdims=True).astype(jnp.int32)
        picked = jnp.concatenate([tiles[t] for t, _ in pairs], axis=1)
        moved = jnp.dot(onehot(place == label), picked, preferred_element_type=F32)
        for n, (_, f) in enumerate(pairs):
            parts.setdefault(f, []).append(moved[:, n * LANES : (n + 1) * LANES])
    for f in sorted(parts):
        whole = functools.reduce(lambda a, b: a + b, parts[f])
        out_ref[0:tok, f * LANES : (f + 1) * LANES] = whole.astype(BF)
    out_ref[tok : tok + 64, :] = w_ref[0:64, :]
    last = w_ref[64:HD, :].astype(F32)
    out_ref[tok + 64 : tok + WROWS, :] = jnp.concatenate([last, last], axis=0).astype(BF)


TOK = 192
WROWS = 80
STEP = 4
QT = 256
KT = 1024
SIDE = 1
VROWS = 80
AROWS = 112
NEG = -3e38
LIMIT = pltpu.CompilerParams(vmem_limit_bytes=56 * 2**20)


def attend_kernel(steps, n_seq, doc_ref, x_ref, w_ref, out_ref, q_s, k_s, v_s, o_s, bound_s):
    step = pl.program_id(0)
    count = STEP * TOK
    start = pl.multiple_of(step * count, count)
    x = x_ref[...].reshape(count, x_ref.shape[2])
    qkv = lax.dot_general(x, w_ref[...], NT, preferred_element_type=F32)
    q_s[pl.ds(start, count), :] = (qkv[:, 0:HD] * (1.0 / math.sqrt(HD))).astype(BF)
    k_s[pl.ds(start, count), :] = qkv[:, HD : 2 * HD].astype(BF)
    turned = qkv[:, LANES : 3 * HD].T[2 * HD - LANES :, :]
    ones = jnp.ones((VROWS - HD, count), F32)
    v_s[:, pl.ds(start, count)] = jnp.concatenate([turned, ones], axis=0).astype(BF)

    @pl.when(step == steps - 1)
    def _():
        length = q_s.shape[0]
        blocks = length // BLK
        per_q = QT // BLK
        per_k = KT // BLK
        k_s[length:, :] = jnp.zeros((KT, HD), BF)
        v_s[:, length:] = jnp.zeros((VROWS, KT), BF)
        first = jnp.int32(0)
        for b in range(blocks):
            if b:
                first = jnp.where(doc_ref[0, b * BLK] == doc_ref[0, (b - 1) * BLK], first, b)
            bound_s[0, b] = first
        last = jnp.int32(blocks)
        for b in reversed(range(blocks)):
            if b < blocks - 1:
                last = jnp.where(doc_ref[0, b * BLK] == doc_ref[0, (b + 1) * BLK], last, b + 1)
            bound_s[1, b] = last

        def some_tiles(group, _):
            tiles = []
            for u in range(SIDE):
                t = group * SIDE + u
                bounds = [
                    (bound_s[0, t * per_q + i], bound_s[1, t * per_q + i]) for i in range(per_q)
                ]
                q = q_s[pl.ds(pl.multiple_of(t * QT, QT), QT), :]
                tiles.append((t, q, bounds))
            chunks = functools.reduce(
                jnp.maximum, [b[-1][1] - b[0][0] for _, _, b in tiles]
            )
            chunks = (chunks + per_k - 1) // per_k

            def one_chunk(c, carry):
                result = []
                for (_, q, bounds), (high, total) in zip(tiles, carry):
                    begin = bounds[0][0] + c * per_k
                    keys = pl.ds(pl.multiple_of(jnp.minimum(begin, blocks) * BLK, BLK), KT)
                    scores = lax.dot_general(k_s[keys, :], q, NT, preferred_element_type=F32)
                    columns = []
                    for i, (lo, hi) in enumerate(bounds):
                        kept = [
                            jnp.where(
                                (begin + j >= lo) & (begin + j < hi),
                                scores[j * BLK : (j + 1) * BLK, i * BLK : (i + 1) * BLK],
                                -jnp.inf,
                            )
                            for j in range(per_k)
                        ]
                        columns.append(jnp.concatenate(kept, axis=0))
                    scores = jnp.concatenate(columns, axis=1)
                    newer = jnp.maximum(high, jnp.max(scores, axis=0, keepdims=True))
                    expo = jnp.exp(scores - newer).astype(BF)
                    total = total * jnp.exp(high - newer) + jnp.dot(
                        v_s[:, keys], expo, preferred_element_type=F32
                    )
                    result.append((newer, total))
                return tuple(result)

            carry = tuple(
                (jnp.full((1, QT), NEG, F32), jnp.zeros((VROWS, QT), F32)) for _ in range(SIDE)
            )
            for (t, _, _), (_, total) in zip(tiles, lax.fori_loop(0, chunks, one_chunk, carry)):
                o_s[:, pl.ds(pl.multiple_of(t * QT, QT), QT)] = total / total[HD : HD + 1, :]
            return 0

        lax.fori_loop(0, length // (QT * SIDE), some_tiles, 0)
        tok = length // n_seq
        for s in range(n_seq):
            mine = o_s[0:HD, s * tok : (s + 1) * tok]
            rest = mine[:, LANES:tok]
            out_ref[s, 0:64, :] = mine[0:64, 0:LANES].astype(BF)
            out_ref[s, 64:96, :] = jnp.concatenate([rest[0:32], rest[32:64]], axis=1).astype(BF)
            empty = jnp.zeros((HD - 64, 2 * LANES - tok), F32)
            out_ref[s, 96:112, :] = jnp.concatenate(
                [mine[64:HD, 0:LANES], jnp.concatenate([rest[64:HD], empty], axis=1)], axis=0
            ).astype(BF)


def project_kernel(n_seq, in_ref, *refs):
    *w_refs, out_ref = refs
    width = out_ref.shape[1]
    tok = out_ref.shape[0]
    rest = tok - LANES

    def features(begin):
        return in_ref[:, begin : begin + 16, :].reshape(n_seq * 16, LANES)

    tail = features(96).astype(F32)
    upper = (iota(tail.shape, 0) & 15) < 8
    tail_near = jnp.where(upper, tail, 0.0).astype(BF)
    tail_far = jnp.where(upper, 0.0, tail).astype(BF)
    near = jnp.concatenate([features(16 * g) for g in range(4)] + [tail_near], axis=0).T
    first, second = features(64).T, features(80).T
    distant = jnp.concatenate(
        [first[0:rest], second[0:rest], first[rest:], second[rest:], tail_far.T[0:rest]], axis=1
    )
    left = jnp.concatenate([near, distant], axis=0)
    weights = jnp.concatenate([ref[...].reshape(n_seq * 16, width) for ref in w_refs], axis=0)
    out_ref[...] = jnp.dot(left, weights, preferred_element_type=F32).astype(BF)


def whole(*shape):
    return pl.BlockSpec(shape, lambda *_: (0,) * len(shape))


def attend_call(doc_ids, tokens, w_t, n_seq):
    length = n_seq * TOK
    width = tokens.shape[2]
    steps = n_seq // STEP
    return pl.pallas_call(
        functools.partial(attend_kernel, steps, n_seq),
        grid=(steps,),
        out_shape=jax.ShapeDtypeStruct((n_seq, AROWS, LANES), BF),
        in_specs=[
            pl.BlockSpec(memory_space=pltpu.SMEM),
            pl.BlockSpec((STEP, TOK, width), lambda i: (i, 0, 0)),
            whole(*w_t.shape),
        ],
        out_specs=whole(n_seq, AROWS, LANES),
        scratch_shapes=[
            pltpu.VMEM((length, HD), BF),
            pltpu.VMEM((length + KT, HD), BF),
            pltpu.VMEM((VROWS, length + KT), BF),
            pltpu.VMEM((VROWS, length), F32),
            pltpu.SMEM((2, length // BLK), jnp.int32),
        ],
        compiler_params=LIMIT,
        name="attend",
    )(doc_ids, tokens, w_t)


def body(source, destination, doc_ids, w_qkv, w_out):
    n_pack = lax.axis_size("pack")
    n_seq = lax.axis_size("seq")
    tok, width = source.shape[1:]
    outbox = pl.pallas_call(
        functools.partial(pack_kernel, n_pack),
        out_shape=jax.ShapeDtypeStruct((n_pack, TILES * 16, LANES), BF),
        compiler_params=LIMIT,
        name="pack_rows",
    )(destination, source[0])
    inbox = lax.all_to_all(outbox, "pack", split_axis=0, concat_axis=0, tiled=True)
    packed = pl.pallas_call(
        functools.partial(unpack_kernel, n_pack),
        out_shape=jax.ShapeDtypeStruct((tok + WROWS, width), BF),
        compiler_params=LIMIT,
        name="unpack_rows",
    )(inbox, w_out)
    tokens = lax.all_gather(packed, "seq", axis=0, tiled=False)

    attended = attend_call(
        doc_ids, tokens, jnp.transpose(w_qkv, (0, 2, 1)).reshape(3 * HD, width), n_seq
    )
    blocks = lax.all_to_all(attended, "seq", split_axis=0, concat_axis=0, tiled=True)

    def w_spec(group):
        return pl.BlockSpec((n_seq, 16, width), lambda i: (0, tok // 16 + group, 0))

    groups = WROWS // 16
    out = pl.pallas_call(
        functools.partial(project_kernel, n_seq),
        grid=(1,),
        out_shape=jax.ShapeDtypeStruct((tok, width), BF),
        in_specs=[whole(*blocks.shape)] + [w_spec(g) for g in range(groups)],
        out_specs=whole(tok, width),
        compiler_params=LIMIT,
        name="project",
    )(blocks, *[tokens] * groups)
    return out[None]


def solution(mesh):
    placed = (
        P("seq", "pack", None),
        P("seq", "pack"),
        P("pack", None),
        P(None, None, "seq"),
        P("seq", None),
    )
    return jax.shard_map(
        body, mesh=mesh, in_specs=placed, out_specs=P("pack", "seq", None), check_vma=False
    )
```

```python
import functools
import math

import jax
import jax.numpy as jnp
from jax import lax
from jax.experimental import pallas as pl
from jax.experimental.pallas import tpu as pltpu
from jax.sharding import PartitionSpec as P

HD = 72
CAP = 12
LANES = 128
BLK = 128
BF = jnp.bfloat16
F32 = jnp.float32
NT = (((1,), (1,)), ((), ()))

SHIFTS = (
    (0, ((0, 0), (3, 4), (6, 8))),
    (-12, ((0, 1), (3, 5))),
    (4, ((1, 1), (4, 5))),
    (-8, ((1, 2), (4, 6))),
    (8, ((2, 2), (5, 6))),
    (-4, ((2, 3), (5, 7))),
)
TILES = 7


def iota(shape, dim):
    return lax.broadcasted_iota(jnp.int32, shape, dim)


def onehot(condition):
    return jnp.where(condition, 1.0, 0.0).astype(BF)


def pack_kernel(n_pack, dest_ref, rows_ref, out_ref):
    tok = rows_ref.shape[0]
    group = n_pack * 16
    dest = dest_ref[...]
    owner = ((dest >> 6) * 171) >> 9
    place = dest - owner * tok
    owned = iota((n_pack, tok), 0) == owner
    before = onehot(iota((tok, tok), 0) < iota((tok, tok), 1))
    counted = jnp.dot(onehot(owned), before, preferred_element_type=F32)
    slot = jnp.sum(jnp.where(owned, counted, 0.0), axis=0, keepdims=True).astype(jnp.int32)
    row = iota((group, tok), 0)
    parts = {}
    for shift, pairs in SHIFTS:
        at = slot - shift
        key = jnp.where((at >= 0) & (at < 16), owner * 16 + at, -1)
        picked = jnp.concatenate(
            [rows_ref[:, f * LANES : (f + 1) * LANES] for _, f in pairs], axis=1
        )
        moved = jnp.dot(onehot(row == key), picked, preferred_element_type=F32)
        for n, (tile, _) in enumerate(pairs):
            parts.setdefault(tile, []).append(moved[:, n * LANES : (n + 1) * LANES])
    tags = jnp.where(iota((LANES, tok), 0) == slot, (place + 1).astype(F32), 0.0).astype(BF)
    here = onehot(row == owner * 16 + CAP)
    parts[TILES - 1].append(lax.dot_general(here, tags, NT, preferred_element_type=F32))
    for tile in range(TILES):
        whole = functools.reduce(lambda a, b: a + b, parts[tile])
        out_ref[:, tile * 16 : (tile + 1) * 16, :] = whole.astype(BF).reshape(n_pack, 16, LANES)


def unpack_kernel(n_pack, in_ref, *refs):
    out_ref = refs[-1]
    tok = out_ref.shape[0]
    group = n_pack * 16
    tiles = [in_ref[:, t * 16 : (t + 1) * 16, :].reshape(group, LANES) for t in range(TILES)]
    col = iota((n_pack, group), 1)
    lead = iota((n_pack, group), 0) * 16
    labels = jnp.dot(onehot(col == lead + CAP), tiles[-1], preferred_element_type=F32).astype(BF)
    mine = (col >= lead) & (col < lead + 16)
    offset = iota((LANES, group), 0) - (iota((LANES, group), 1) & 15)
    place = iota((tok, group), 0) + 1
    parts = {}
    for shift, pairs in SHIFTS:
        spread = jnp.dot(labels, onehot(offset == shift), preferred_element_type=F32)
        label = jnp.sum(jnp.where(mine, spread, 0.0), axis=0, keepdims=True).astype(jnp.int32)
        picked = jnp.concatenate([tiles[t] for t, _ in pairs], axis=1)
        moved = jnp.dot(onehot(place == label), picked, preferred_element_type=F32)
        for n, (_, f) in enumerate(pairs):
            parts.setdefault(f, []).append(moved[:, n * LANES : (n + 1) * LANES])
    for f in sorted(parts):
        whole = functools.reduce(lambda a, b: a + b, parts[f])
        out_ref[:, f * LANES : (f + 1) * LANES] = whole.astype(BF)


TOK = 192
QT = 768
KT = 1024
SIDE = 1
VROWS = 80
QKV = 256
AROWS = 112
NEG = -3e38
BACK = (0, 1, -1, 2, -2, 3, -3, 4)
LIMIT = pltpu.CompilerParams(vmem_limit_bytes=56 * 2**20)


def origin(me, n):
    chips = len(BACK)
    core = me & 1
    chip = ((me >> 1) - BACK[n % chips]) & (chips - 1)
    return 2 * chip + (core if n < chips else 1 - core)


def qkv_kernel(*refs):
    *x_refs, mine_w_ref, pair_w_ref, mine_ref, pair_ref = refs
    x = jnp.concatenate([ref[...] for ref in x_refs], axis=0)
    rows = x.shape[0]
    scale = jnp.where(iota((1, 3 * HD), 1) < HD, 1.0 / math.sqrt(HD), 1.0)
    fill = jnp.where(iota((rows, QKV - 3 * HD), 1) < VROWS - HD, 1.0, 0.0)
    for w_ref, out_ref in ((mine_w_ref, mine_ref), (pair_w_ref, pair_ref)):
        qkv = lax.dot_general(x, w_ref[...], NT, preferred_element_type=F32) * scale
        whole = jnp.concatenate([qkv, fill], axis=1).astype(BF)
        out_ref[...] = whole.reshape(rows // TOK, TOK, QKV)


def attend_kernel(n_seq, me_ref, doc_ref, *refs):
    *in_refs, out_ref, q_s, k_s, row_s, v_s, o_s, bound_s = refs
    n = 0
    for ref in in_refs:
        for i in range(ref.shape[0]):
            rows = pl.ds(pl.multiple_of(origin(me_ref[0], n) * TOK, 64), TOK)
            q_s[rows, :] = ref[i, :, 0:HD]
            k_s[rows, :] = ref[i, :, HD : 2 * HD]
            row_s[rows, :] = ref[i, :, LANES:QKV]
            n += 1
    length = q_s.shape[0]
    blocks = length // BLK
    per_q = QT // BLK
    per_k = KT // BLK
    for b in range(blocks):
        turned = row_s[b * BLK : (b + 1) * BLK, :].T
        begin = 2 * HD - LANES
        v_s[:, b * BLK : (b + 1) * BLK] = turned[begin : begin + VROWS, :]
    k_s[length:, :] = jnp.zeros((KT, HD), BF)
    v_s[:, length:] = jnp.zeros((VROWS, KT), BF)
    first = jnp.int32(0)
    for b in range(blocks):
        if b:
            first = jnp.where(doc_ref[0, b * BLK] == doc_ref[0, (b - 1) * BLK], first, b)
        bound_s[0, b] = first
    last = jnp.int32(blocks)
    for b in reversed(range(blocks)):
        if b < blocks - 1:
            last = jnp.where(doc_ref[0, b * BLK] == doc_ref[0, (b + 1) * BLK], last, b + 1)
        bound_s[1, b] = last

    def some_tiles(group, _):
        tiles = []
        for u in range(SIDE):
            t = group * SIDE + u
            bounds = [
                (bound_s[0, t * per_q + i], bound_s[1, t * per_q + i]) for i in range(per_q)
            ]
            q = q_s[pl.ds(pl.multiple_of(t * QT, QT), QT), :]
            tiles.append((t, q, bounds))
        chunks = functools.reduce(
            jnp.maximum, [b[-1][1] - b[0][0] for _, _, b in tiles]
        )
        chunks = (chunks + per_k - 1) // per_k

        def one_chunk(c, carry):
            result = []
            for (_, q, bounds), (high, total) in zip(tiles, carry):
                begin = bounds[0][0] + c * per_k
                keys = pl.ds(pl.multiple_of(jnp.minimum(begin, blocks) * BLK, BLK), KT)
                scores = lax.dot_general(k_s[keys, :], q, NT, preferred_element_type=F32)
                columns = []
                for i, (lo, hi) in enumerate(bounds):
                    kept = [
                        jnp.where(
                            (begin + j >= lo) & (begin + j < hi),
                            scores[j * BLK : (j + 1) * BLK, i * BLK : (i + 1) * BLK],
                            -jnp.inf,
                        )
                        for j in range(per_k)
                    ]
                    columns.append(jnp.concatenate(kept, axis=0))
                scores = jnp.concatenate(columns, axis=1)
                newer = jnp.maximum(high, jnp.max(scores, axis=0, keepdims=True))
                expo = jnp.exp(scores - newer).astype(BF)
                total = total * jnp.exp(high - newer) + jnp.dot(
                    v_s[:, keys], expo, preferred_element_type=F32
                )
                result.append((newer, total))
            return tuple(result)

        carry = tuple(
            (jnp.full((1, QT), NEG, F32), jnp.zeros((VROWS, QT), F32)) for _ in range(SIDE)
        )
        for (t, _, _), (_, total) in zip(tiles, lax.fori_loop(0, chunks, one_chunk, carry)):
            o_s[:, pl.ds(pl.multiple_of(t * QT, QT), QT)] = total / total[HD : HD + 1, :]
        return 0

    lax.fori_loop(0, length // (QT * SIDE), some_tiles, 0)
    tok = length // n_seq
    for s in range(n_seq):
        mine = o_s[0:HD, s * tok : (s + 1) * tok]
        rest = mine[:, LANES:tok]
        out_ref[s, 0:64, :] = mine[0:64, 0:LANES].astype(BF)
        out_ref[s, 64:96, :] = jnp.concatenate([rest[0:32], rest[32:64]], axis=1).astype(BF)
        empty = jnp.zeros((HD - 64, 2 * LANES - tok), F32)
        out_ref[s, 96:112, :] = jnp.concatenate(
            [mine[64:HD, 0:LANES], jnp.concatenate([rest[64:HD], empty], axis=1)], axis=0
        ).astype(BF)


def project_kernel(n_seq, in_ref, w_ref, out_ref):
    width = out_ref.shape[1]
    tok = out_ref.shape[0]
    rest = tok - LANES
    lo = in_ref[:, 0:32, :].reshape(n_seq * 32, LANES)
    hi = in_ref[:, 32:64, :].reshape(n_seq * 32, LANES)
    far = in_ref[:, 64:96, :].reshape(n_seq * 32, LANES)
    tail = in_ref[:, 96:112, :].reshape(n_seq * 16, LANES).astype(F32)
    upper = (iota(tail.shape, 0) & 15) < 8
    tail_near = jnp.where(upper, tail, 0.0).astype(BF)
    tail_far = jnp.where(upper, 0.0, tail).astype(BF)
    near = jnp.concatenate([lo, hi, tail_near], axis=0).T
    far_t = far.T
    distant = jnp.concatenate([far_t[0:rest], far_t[rest:LANES], tail_far.T[0:rest]], axis=1)
    left = jnp.concatenate([near, distant], axis=0)
    last = w_ref[:, 64:HD, :].astype(F32)
    weights = jnp.concatenate(
        [
            w_ref[:, 0:32, :].reshape(n_seq * 32, width),
            w_ref[:, 32:64, :].reshape(n_seq * 32, width),
            jnp.concatenate([last, last], axis=1).reshape(n_seq * 16, width).astype(BF),
        ],
        axis=0,
    )
    out_ref[...] = jnp.dot(left, weights, preferred_element_type=F32).astype(BF)


def cost(flops, operands, out_shape):
    total = sum(math.prod(x.shape) * x.dtype.itemsize for x in operands)
    total += sum(math.prod(x.shape) * x.dtype.itemsize for x in jax.tree.leaves(out_shape))
    return pl.CostEstimate(flops=flops, bytes_accessed=total, transcendentals=0)


def local_call(kernel, out_shape, *operands, name, flops, small=0, scratch=(), behind=()):
    smem = pl.BlockSpec(memory_space=pltpu.SMEM)
    vmem = pl.BlockSpec(memory_space=pltpu.VMEM)
    after = [pl.BlockSpec(memory_space=pl.ANY)] * len(behind)
    return pl.pallas_call(
        kernel,
        out_shape=out_shape,
        in_specs=[smem] * small + [vmem] * (len(operands) - small) + after,
        out_specs=jax.tree.map(lambda _: vmem, out_shape),
        scratch_shapes=scratch,
        compiler_params=LIMIT,
        cost_estimate=cost(flops, operands, out_shape),
        name=name,
    )(*operands, *behind)


def project_qkv(blocks, mine_w, pair_w, name):
    rows = sum(x.shape[0] for x in blocks)
    out = jax.ShapeDtypeStruct((rows // TOK, TOK, QKV), BF)
    flops = 2 * rows * mine_w.shape[1] * 6 * HD
    return local_call(
        qkv_kernel, (out, out), *blocks, mine_w, pair_w, name=name, flops=flops
    )


def attend_call(me, doc_ids, n_seq, *blocks):
    length = n_seq * TOK
    return local_call(
        functools.partial(attend_kernel, n_seq),
        jax.ShapeDtypeStruct((n_seq, AROWS, LANES), BF),
        me,
        doc_ids,
        *blocks,
        small=2,
        flops=2 * length * length * HD,
        scratch=[
            pltpu.VMEM((length, HD), BF),
            pltpu.VMEM((length + KT, HD), BF),
            pltpu.VMEM((length, LANES), BF),
            pltpu.VMEM((VROWS, length + KT), BF),
            pltpu.VMEM((VROWS, length), F32),
            pltpu.SMEM((2, length // BLK), jnp.int32),
        ],
        name="attend",
    )


def ring_step(right, left, n_seq):
    up = [(i, (i + 2) % n_seq) for i in range(n_seq)]
    down = [(i, (i - 2) % n_seq) for i in range(n_seq)]
    return lax.ppermute(right, "seq", up), lax.ppermute(left, "seq", down)


def body(source, destination, doc_ids, w_qkv, w_out):
    n_pack = lax.axis_size("pack")
    n_seq = lax.axis_size("seq")
    width = source.shape[2]
    shape = jax.ShapeDtypeStruct
    me = lax.axis_index("seq").astype(jnp.int32).reshape(1)
    w_t = jnp.transpose(w_qkv, (0, 2, 1)).reshape(3 * HD, width)

    def other_core(x):
        return lax.ppermute(x, "seq", [(i, i ^ 1) for i in range(n_seq)])

    outbox = local_call(
        functools.partial(pack_kernel, n_pack),
        shape((n_pack, TILES * 16, LANES), BF),
        destination,
        source[0],
        name="pack_rows",
        flops=10**9,
    )
    inbox = lax.all_to_all(outbox, "pack", split_axis=0, concat_axis=0, tiled=True)

    pair_w = other_core(w_t)
    w_all = lax.all_gather(w_out, "seq", axis=0, tiled=False)

    packed = local_call(
        functools.partial(unpack_kernel, n_pack),
        shape((TOK, width), BF),
        inbox,
        name="unpack_rows",
        flops=10**9,
        behind=(pair_w,),
    )
    right = left = packed
    held = [packed]
    for _ in range(3):
        right, left = ring_step(right, left, n_seq)
        held += [right, left]
    held += ring_step(right[: TOK // 2], left[TOK // 2 :], n_seq)

    mine, theirs = [], []
    for n, (begin, end) in enumerate(((0, 5), (5, 9))):
        own, other = project_qkv(held[begin:end], w_t, pair_w, f"qkv_{n}")
        mine.append(own)
        theirs.append(other_core(other))
    attended = attend_call(me, doc_ids, n_seq, *mine, *theirs)
    blocks = lax.all_to_all(attended, "seq", split_axis=0, concat_axis=0, tiled=True)

    out = local_call(
        functools.partial(project_kernel, n_seq),
        shape((TOK, width), BF),
        blocks,
        w_all,
        name="project",
        flops=2 * TOK * width * width,
    )
    return out[None]


def solution(mesh):
    placed = (
        P("seq", "pack", None),
        P("seq", "pack"),
        P("pack", None),
        P(None, None, "seq"),
        P("seq", None),
    )
    return jax.shard_map(
        body, mesh=mesh, in_specs=placed, out_specs=P("pack", "seq", None), check_vma=False
    )
```

```python
import functools
import math

import jax
import jax.numpy as jnp
from jax import lax
from jax.experimental import pallas as pl
from jax.experimental.pallas import tpu as pltpu
from jax.sharding import PartitionSpec as P

HD = 72
CAP = 12
LANES = 128
BLK = 128
BF = jnp.bfloat16
F32 = jnp.float32
NT = (((1,), (1,)), ((), ()))

SHIFTS = (
    (0, ((0, 0), (3, 4), (6, 8))),
    (-12, ((0, 1), (3, 5))),
    (4, ((1, 1), (4, 5))),
    (-8, ((1, 2), (4, 6))),
    (8, ((2, 2), (5, 6))),
    (-4, ((2, 3), (5, 7))),
)
TILES = 7


def iota(shape, dim):
    return lax.broadcasted_iota(jnp.int32, shape, dim)


def onehot(condition):
    return jnp.where(condition, 1.0, 0.0).astype(BF)


def pack_kernel(n_pack, dest_ref, rows_ref, out_ref):
    tok = rows_ref.shape[0]
    group = n_pack * 16
    dest = dest_ref[...]
    owner = ((dest >> 6) * 171) >> 9
    place = dest - owner * tok
    owned = iota((n_pack, tok), 0) == owner
    before = onehot(iota((tok, tok), 0) < iota((tok, tok), 1))
    counted = jnp.dot(onehot(owned), before, preferred_element_type=F32)
    slot = jnp.sum(jnp.where(owned, counted, 0.0), axis=0, keepdims=True).astype(jnp.int32)
    row = iota((group, tok), 0)
    parts = {}
    for shift, pairs in SHIFTS:
        at = slot - shift
        key = jnp.where((at >= 0) & (at < 16), owner * 16 + at, -1)
        picked = jnp.concatenate(
            [rows_ref[:, f * LANES : (f + 1) * LANES] for _, f in pairs], axis=1
        )
        moved = jnp.dot(onehot(row == key), picked, preferred_element_type=F32)
        for n, (tile, _) in enumerate(pairs):
            parts.setdefault(tile, []).append(moved[:, n * LANES : (n + 1) * LANES])
    tags = jnp.where(iota((LANES, tok), 0) == slot, (place + 1).astype(F32), 0.0).astype(BF)
    here = onehot(row == owner * 16 + CAP)
    parts[TILES - 1].append(lax.dot_general(here, tags, NT, preferred_element_type=F32))
    for tile in range(TILES):
        whole = functools.reduce(lambda a, b: a + b, parts[tile])
        out_ref[:, tile * 16 : (tile + 1) * 16, :] = whole.astype(BF).reshape(n_pack, 16, LANES)


def unpack_kernel(n_pack, in_ref, *refs):
    out_ref = refs[-1]
    tok = out_ref.shape[0]
    group = n_pack * 16
    tiles = [in_ref[:, t * 16 : (t + 1) * 16, :].reshape(group, LANES) for t in range(TILES)]
    col = iota((n_pack, group), 1)
    lead = iota((n_pack, group), 0) * 16
    labels = jnp.dot(onehot(col == lead + CAP), tiles[-1], preferred_element_type=F32).astype(BF)
    mine = (col >= lead) & (col < lead + 16)
    offset = iota((LANES, group), 0) - (iota((LANES, group), 1) & 15)
    place = iota((tok, group), 0) + 1
    parts = {}
    for shift, pairs in SHIFTS:
        spread = jnp.dot(labels, onehot(offset == shift), preferred_element_type=F32)
        label = jnp.sum(jnp.where(mine, spread, 0.0), axis=0, keepdims=True).astype(jnp.int32)
        picked = jnp.concatenate([tiles[t] for t, _ in pairs], axis=1)
        moved = jnp.dot(onehot(place == label), picked, preferred_element_type=F32)
        for n, (_, f) in enumerate(pairs):
            parts.setdefault(f, []).append(moved[:, n * LANES : (n + 1) * LANES])
    for f in sorted(parts):
        whole = functools.reduce(lambda a, b: a + b, parts[f])
        out_ref[:, f * LANES : (f + 1) * LANES] = whole.astype(BF)


TOK = 192
QT = 768
KT = 1024
SIDE = 1
VROWS = 80
QKV = 256
AROWS = 112
NEG = -3e38
BACK = (0, 1, -1, 2, -2, 3, -3, 4)
LIMIT = pltpu.CompilerParams(vmem_limit_bytes=30 * 2**20)


def origin(me, n):
    chips = len(BACK)
    core = me & 1
    chip = ((me >> 1) - BACK[n % chips]) & (chips - 1)
    return 2 * chip + (core if n < chips else 1 - core)


def qkv_kernel(*refs):
    *x_refs, mine_w_ref, pair_w_ref, mine_ref, pair_ref = refs
    x = jnp.concatenate([ref[...] for ref in x_refs], axis=0)
    rows = x.shape[0]
    scale = jnp.where(iota((1, 3 * HD), 1) < HD, 1.0 / math.sqrt(HD), 1.0)
    fill = jnp.where(iota((rows, QKV - 3 * HD), 1) < VROWS - HD, 1.0, 0.0)
    for w_ref, out_ref in ((mine_w_ref, mine_ref), (pair_w_ref, pair_ref)):
        qkv = lax.dot_general(x, w_ref[...], NT, preferred_element_type=F32) * scale
        whole = jnp.concatenate([qkv, fill], axis=1).astype(BF)
        out_ref[...] = whole.reshape(rows // TOK, TOK, QKV)


def attend_kernel(n_seq, me_ref, doc_ref, *refs):
    *in_refs, out_ref, q_s, k_s, row_s, v_s, o_s, bound_s = refs
    n = 0
    for ref in in_refs:
        for i in range(ref.shape[0]):
            rows = pl.ds(pl.multiple_of(origin(me_ref[0], n) * TOK, 64), TOK)
            q_s[rows, :] = ref[i, :, 0:HD]
            k_s[rows, :] = ref[i, :, HD : 2 * HD]
            row_s[rows, :] = ref[i, :, LANES:QKV]
            n += 1
    length = q_s.shape[0]
    blocks = length // BLK
    per_q = QT // BLK
    per_k = KT // BLK
    for b in range(blocks):
        turned = row_s[b * BLK : (b + 1) * BLK, :].T
        begin = 2 * HD - LANES
        v_s[:, b * BLK : (b + 1) * BLK] = turned[begin : begin + VROWS, :]
    k_s[length:, :] = jnp.zeros((KT, HD), BF)
    v_s[:, length:] = jnp.zeros((VROWS, KT), BF)
    first = jnp.int32(0)
    for b in range(blocks):
        if b:
            first = jnp.where(doc_ref[0, b * BLK] == doc_ref[0, (b - 1) * BLK], first, b)
        bound_s[0, b] = first
    last = jnp.int32(blocks)
    for b in reversed(range(blocks)):
        if b < blocks - 1:
            last = jnp.where(doc_ref[0, b * BLK] == doc_ref[0, (b + 1) * BLK], last, b + 1)
        bound_s[1, b] = last

    def some_tiles(group, _):
        tiles = []
        for u in range(SIDE):
            t = group * SIDE + u
            bounds = [
                (bound_s[0, t * per_q + i], bound_s[1, t * per_q + i]) for i in range(per_q)
            ]
            q = q_s[pl.ds(pl.multiple_of(t * QT, QT), QT), :]
            tiles.append((t, q, bounds))
        chunks = functools.reduce(
            jnp.maximum, [b[-1][1] - b[0][0] for _, _, b in tiles]
        )
        chunks = (chunks + per_k - 1) // per_k

        def one_chunk(c, carry):
            result = []
            for (_, q, bounds), (high, total) in zip(tiles, carry):
                begin = bounds[0][0] + c * per_k
                keys = pl.ds(pl.multiple_of(jnp.minimum(begin, blocks) * BLK, BLK), KT)
                scores = lax.dot_general(k_s[keys, :], q, NT, preferred_element_type=F32)
                columns = []
                for i, (lo, hi) in enumerate(bounds):
                    kept = [
                        jnp.where(
                            (begin + j >= lo) & (begin + j < hi),
                            scores[j * BLK : (j + 1) * BLK, i * BLK : (i + 1) * BLK],
                            -jnp.inf,
                        )
                        for j in range(per_k)
                    ]
                    columns.append(jnp.concatenate(kept, axis=0))
                scores = jnp.concatenate(columns, axis=1)
                newer = jnp.maximum(high, jnp.max(scores, axis=0, keepdims=True))
                expo = jnp.exp(scores - newer).astype(BF)
                total = total * jnp.exp(high - newer) + jnp.dot(
                    v_s[:, keys], expo, preferred_element_type=F32
                )
                result.append((newer, total))
            return tuple(result)

        carry = tuple(
            (jnp.full((1, QT), NEG, F32), jnp.zeros((VROWS, QT), F32)) for _ in range(SIDE)
        )
        for (t, _, _), (_, total) in zip(tiles, lax.fori_loop(0, chunks, one_chunk, carry)):
            o_s[:, pl.ds(pl.multiple_of(t * QT, QT), QT)] = total / total[HD : HD + 1, :]
        return 0

    lax.fori_loop(0, length // (QT * SIDE), some_tiles, 0)
    tok = length // n_seq
    for s in range(n_seq):
        mine = o_s[0:HD, s * tok : (s + 1) * tok]
        rest = mine[:, LANES:tok]
        out_ref[s, 0:64, :] = mine[0:64, 0:LANES].astype(BF)
        out_ref[s, 64:96, :] = jnp.concatenate([rest[0:32], rest[32:64]], axis=1).astype(BF)
        empty = jnp.zeros((HD - 64, 2 * LANES - tok), F32)
        out_ref[s, 96:112, :] = jnp.concatenate(
            [mine[64:HD, 0:LANES], jnp.concatenate([rest[64:HD], empty], axis=1)], axis=0
        ).astype(BF)


def project_kernel(n_seq, in_ref, w_ref, out_ref):
    width = out_ref.shape[1]
    tok = out_ref.shape[0]
    rest = tok - LANES
    lo = in_ref[:, 0:32, :].reshape(n_seq * 32, LANES)
    hi = in_ref[:, 32:64, :].reshape(n_seq * 32, LANES)
    far = in_ref[:, 64:96, :].reshape(n_seq * 32, LANES)
    tail = in_ref[:, 96:112, :].reshape(n_seq * 16, LANES).astype(F32)
    upper = (iota(tail.shape, 0) & 15) < 8
    tail_near = jnp.where(upper, tail, 0.0).astype(BF)
    tail_far = jnp.where(upper, 0.0, tail).astype(BF)
    near = jnp.concatenate([lo, hi, tail_near], axis=0).T
    far_t = far.T
    distant = jnp.concatenate([far_t[0:rest], far_t[rest:LANES], tail_far.T[0:rest]], axis=1)
    left = jnp.concatenate([near, distant], axis=0)
    last = w_ref[:, 64:HD, :].astype(F32)
    weights = jnp.concatenate(
        [
            w_ref[:, 0:32, :].reshape(n_seq * 32, width),
            w_ref[:, 32:64, :].reshape(n_seq * 32, width),
            jnp.concatenate([last, last], axis=1).reshape(n_seq * 16, width).astype(BF),
        ],
        axis=0,
    )
    out_ref[...] = jnp.dot(left, weights, preferred_element_type=F32).astype(BF)


def cost(flops, operands, out_shape):
    total = sum(math.prod(x.shape) * x.dtype.itemsize for x in operands)
    total += sum(math.prod(x.shape) * x.dtype.itemsize for x in jax.tree.leaves(out_shape))
    return pl.CostEstimate(flops=flops, bytes_accessed=total, transcendentals=0)


def local_call(kernel, out_shape, *operands, name, flops, small=0, scratch=(), behind=()):
    smem = pl.BlockSpec(memory_space=pltpu.SMEM)
    vmem = pl.BlockSpec(memory_space=pltpu.VMEM)
    after = [pl.BlockSpec(memory_space=pl.ANY)] * len(behind)
    return pl.pallas_call(
        kernel,
        out_shape=out_shape,
        in_specs=[smem] * small + [vmem] * (len(operands) - small) + after,
        out_specs=jax.tree.map(lambda _: vmem, out_shape),
        scratch_shapes=scratch,
        compiler_params=LIMIT,
        cost_estimate=cost(flops, operands, out_shape),
        name=name,
    )(*operands, *behind)


def project_qkv(blocks, mine_w, pair_w, name):
    rows = sum(x.shape[0] for x in blocks)
    out = jax.ShapeDtypeStruct((rows // TOK, TOK, QKV), BF)
    flops = 2 * rows * mine_w.shape[1] * 6 * HD
    return local_call(
        qkv_kernel, (out, out), *blocks, mine_w, pair_w, name=name, flops=flops
    )


def attend_call(me, doc_ids, n_seq, *blocks):
    length = n_seq * TOK
    return local_call(
        functools.partial(attend_kernel, n_seq),
        jax.ShapeDtypeStruct((n_seq, AROWS, LANES), BF),
        me,
        doc_ids,
        *blocks,
        small=2,
        flops=2 * length * length * HD,
        scratch=[
            pltpu.VMEM((length, HD), BF),
            pltpu.VMEM((length + KT, HD), BF),
            pltpu.VMEM((length, LANES), BF),
            pltpu.VMEM((VROWS, length + KT), BF),
            pltpu.VMEM((VROWS, length), F32),
            pltpu.SMEM((2, length // BLK), jnp.int32),
        ],
        name="attend",
    )


def halves_kernel(right_ref, left_ref, *refs):
    *_, top_ref, bottom_ref = refs
    half = top_ref.shape[0]
    top_ref[...] = right_ref[0:half, :]
    bottom_ref[...] = left_ref[half:, :]


def ring_step(right, left, n_seq):
    up = [(i, (i + 2) % n_seq) for i in range(n_seq)]
    down = [(i, (i - 2) % n_seq) for i in range(n_seq)]
    return lax.ppermute(right, "seq", up), lax.ppermute(left, "seq", down)


def body(source, destination, doc_ids, w_qkv, w_out):
    n_pack = lax.axis_size("pack")
    n_seq = lax.axis_size("seq")
    width = source.shape[2]
    shape = jax.ShapeDtypeStruct
    me = lax.axis_index("seq").astype(jnp.int32).reshape(1)
    w_t = jnp.transpose(w_qkv, (0, 2, 1)).reshape(3 * HD, width)

    def other_core(x):
        return lax.ppermute(x, "seq", [(i, i ^ 1) for i in range(n_seq)])

    outbox = local_call(
        functools.partial(pack_kernel, n_pack),
        shape((n_pack, TILES * 16, LANES), BF),
        destination,
        source[0],
        name="pack_rows",
        flops=10**9,
    )
    inbox = lax.all_to_all(outbox, "pack", split_axis=0, concat_axis=0, tiled=True)

    pair_w = other_core(w_t)
    w_all = lax.all_gather(w_out, "seq", axis=0, tiled=False)

    packed = local_call(
        functools.partial(unpack_kernel, n_pack),
        shape((TOK, width), BF),
        inbox,
        name="unpack_rows",
        flops=10**9,
        behind=(pair_w,),
    )
    right = left = packed
    held = [packed]
    for _ in range(3):
        right, left = ring_step(right, left, n_seq)
        held += [right, left]
    mine, theirs = project_qkv(held[:5], w_t, pair_w, "qkv_first")
    half = shape((TOK // 2, width), BF)
    top, bottom = local_call(
        halves_kernel, (half, half), right, left, behind=(theirs,), name="halves", flops=0
    )
    held += ring_step(top, bottom, n_seq)
    last_mine, last_theirs = project_qkv(held[5:], w_t, pair_w, "qkv_last")
    ours = [mine, last_mine, other_core(theirs), other_core(last_theirs)]
    attended = attend_call(me, doc_ids, n_seq, *ours)
    blocks = lax.all_to_all(attended, "seq", split_axis=0, concat_axis=0, tiled=True)

    out = local_call(
        functools.partial(project_kernel, n_seq),
        shape((TOK, width), BF),
        blocks,
        w_all,
        name="project",
        flops=2 * TOK * width * width,
    )
    return out[None]


def solution(mesh):
    placed = (
        P("seq", "pack", None),
        P("seq", "pack"),
        P("pack", None),
        P(None, None, "seq"),
        P("seq", None),
    )
    return jax.shard_map(
        body, mesh=mesh, in_specs=placed, out_specs=P("pack", "seq", None), check_vma=False
    )
```

```python
import functools
import math

import jax
import jax.numpy as jnp
from jax import lax
from jax.experimental import pallas as pl
from jax.experimental.pallas import tpu as pltpu
from jax.sharding import PartitionSpec as P

HD = 72
CAP = 12
LANES = 128
BLK = 128
BF = jnp.bfloat16
F32 = jnp.float32
NT = (((1,), (1,)), ((), ()))

SHIFTS = (
    (0, ((0, 0), (3, 4), (6, 8))),
    (-12, ((0, 1), (3, 5))),
    (4, ((1, 1), (4, 5))),
    (-8, ((1, 2), (4, 6))),
    (8, ((2, 2), (5, 6))),
    (-4, ((2, 3), (5, 7))),
)
TILES = 7


def iota(shape, dim):
    return lax.broadcasted_iota(jnp.int32, shape, dim)


def onehot(condition):
    return jnp.where(condition, 1.0, 0.0).astype(BF)


def pack_kernel(n_pack, dest_ref, rows_ref, out_ref):
    tok = rows_ref.shape[0]
    group = n_pack * 16
    dest = dest_ref[...]
    owner = ((dest >> 6) * 171) >> 9
    place = dest - owner * tok
    owned = iota((n_pack, tok), 0) == owner
    before = onehot(iota((tok, tok), 0) < iota((tok, tok), 1))
    counted = jnp.dot(onehot(owned), before, preferred_element_type=F32)
    slot = jnp.sum(jnp.where(owned, counted, 0.0), axis=0, keepdims=True).astype(jnp.int32)
    row = iota((group, tok), 0)
    parts = {}
    for shift, pairs in SHIFTS:
        at = slot - shift
        key = jnp.where((at >= 0) & (at < 16), owner * 16 + at, -1)
        picked = jnp.concatenate(
            [rows_ref[:, f * LANES : (f + 1) * LANES] for _, f in pairs], axis=1
        )
        moved = jnp.dot(onehot(row == key), picked, preferred_element_type=F32)
        for n, (tile, _) in enumerate(pairs):
            parts.setdefault(tile, []).append(moved[:, n * LANES : (n + 1) * LANES])
    tags = jnp.where(iota((LANES, tok), 0) == slot, (place + 1).astype(F32), 0.0).astype(BF)
    here = onehot(row == owner * 16 + CAP)
    parts[TILES - 1].append(lax.dot_general(here, tags, NT, preferred_element_type=F32))
    for tile in range(TILES):
        whole = functools.reduce(lambda a, b: a + b, parts[tile])
        out_ref[:, tile * 16 : (tile + 1) * 16, :] = whole.astype(BF).reshape(n_pack, 16, LANES)


def unpack_kernel(n_pack, in_ref, *refs):
    out_ref = refs[-1]
    tok = out_ref.shape[0]
    group = n_pack * 16
    tiles = [in_ref[:, t * 16 : (t + 1) * 16, :].reshape(group, LANES) for t in range(TILES)]
    col = iota((n_pack, group), 1)
    lead = iota((n_pack, group), 0) * 16
    labels = jnp.dot(onehot(col == lead + CAP), tiles[-1], preferred_element_type=F32).astype(BF)
    mine = (col >= lead) & (col < lead + 16)
    offset = iota((LANES, group), 0) - (iota((LANES, group), 1) & 15)
    place = iota((tok, group), 0) + 1
    parts = {}
    for shift, pairs in SHIFTS:
        spread = jnp.dot(labels, onehot(offset == shift), preferred_element_type=F32)
        label = jnp.sum(jnp.where(mine, spread, 0.0), axis=0, keepdims=True).astype(jnp.int32)
        picked = jnp.concatenate([tiles[t] for t, _ in pairs], axis=1)
        moved = jnp.dot(onehot(place == label), picked, preferred_element_type=F32)
        for n, (_, f) in enumerate(pairs):
            parts.setdefault(f, []).append(moved[:, n * LANES : (n + 1) * LANES])
    for f in sorted(parts):
        whole = functools.reduce(lambda a, b: a + b, parts[f])
        out_ref[:, f * LANES : (f + 1) * LANES] = whole.astype(BF)


TOK = 192
QT = 768
KT = 1024
SIDE = 1
VROWS = 80
QKV = 256
AROWS = 112
NEG = -3e38
BACK = (0, 1, -1, 2, -2, 3, -3, 4)


def origin(me, n):
    chips = len(BACK)
    core = me & 1
    chip = ((me >> 1) - BACK[n % chips]) & (chips - 1)
    return 2 * chip + (core if n < chips else 1 - core)


def qkv_kernel(*refs):
    *x_refs, mine_w_ref, pair_w_ref, mine_ref, pair_ref = refs
    x = jnp.concatenate([ref[...] for ref in x_refs], axis=0)
    rows = x.shape[0]
    scale = jnp.where(iota((1, 3 * HD), 1) < HD, math.log2(math.e) / math.sqrt(HD), 1.0)
    fill = jnp.where(iota((rows, QKV - 3 * HD), 1) < VROWS - HD, 1.0, 0.0)
    for w_ref, out_ref in ((mine_w_ref, mine_ref), (pair_w_ref, pair_ref)):
        qkv = lax.dot_general(x, w_ref[...], NT, preferred_element_type=F32) * scale
        whole = jnp.concatenate([qkv, fill], axis=1).astype(BF)
        out_ref[...] = whole.reshape(rows // TOK, TOK, QKV)


def attend_kernel(n_seq, me_ref, doc_ref, *refs):
    *in_refs, out_ref, q_s, k_s, row_s, v_s, o_s, bound_s = refs
    n = 0
    for ref in in_refs:
        for i in range(ref.shape[0]):
            rows = pl.ds(pl.multiple_of(origin(me_ref[0], n) * TOK, 64), TOK)
            q_s[rows, :] = ref[i, :, 0:HD]
            k_s[rows, :] = ref[i, :, HD : 2 * HD]
            row_s[rows, :] = ref[i, :, LANES:QKV]
            n += 1
    length = q_s.shape[0]
    blocks = length // BLK
    per_q = QT // BLK
    per_k = KT // BLK
    for b in range(blocks):
        turned = row_s[b * BLK : (b + 1) * BLK, :].T
        begin = 2 * HD - LANES
        v_s[:, b * BLK : (b + 1) * BLK] = turned[begin : begin + VROWS, :]
    k_s[length:, :] = jnp.zeros((KT, HD), BF)
    v_s[:, length:] = jnp.zeros((VROWS, KT), BF)
    first = jnp.int32(0)
    for b in range(blocks):
        if b:
            first = jnp.where(doc_ref[0, b * BLK] == doc_ref[0, (b - 1) * BLK], first, b)
        bound_s[0, b] = first
    last = jnp.int32(blocks)
    for b in reversed(range(blocks)):
        if b < blocks - 1:
            last = jnp.where(doc_ref[0, b * BLK] == doc_ref[0, (b + 1) * BLK], last, b + 1)
        bound_s[1, b] = last

    def some_tiles(group, _):
        tiles = []
        for u in range(SIDE):
            t = group * SIDE + u
            bounds = [
                (bound_s[0, t * per_q + i], bound_s[1, t * per_q + i]) for i in range(per_q)
            ]
            q = q_s[pl.ds(pl.multiple_of(t * QT, QT), QT), :]
            tiles.append((t, q, bounds))
        chunks = functools.reduce(
            jnp.maximum, [b[-1][1] - b[0][0] for _, _, b in tiles]
        )
        big = (chunks + per_k // 2 - 1) // per_k
        small = jnp.where(chunks > big * per_k, 1, 0)

        def one_chunk(width, base, c, carry):
            result = []
            for (_, q, bounds), (high, total) in zip(tiles, carry):
                begin = bounds[0][0] + base + c * (width // BLK)
                keys = pl.ds(pl.multiple_of(jnp.minimum(begin, blocks) * BLK, BLK), width)
                scores = lax.dot_general(k_s[keys, :], q, NT, preferred_element_type=F32)
                columns = []
                for i, (lo, hi) in enumerate(bounds):
                    kept = [
                        jnp.where(
                            (begin + j >= lo) & (begin + j < hi),
                            scores[j * BLK : (j + 1) * BLK, i * BLK : (i + 1) * BLK],
                            -jnp.inf,
                        )
                        for j in range(width // BLK)
                    ]
                    columns.append(jnp.concatenate(kept, axis=0))
                scores = jnp.concatenate(columns, axis=1)
                newer = jnp.maximum(high, jnp.max(scores, axis=0, keepdims=True))
                expo = jnp.exp2(scores - newer).astype(BF)
                total = total * jnp.exp2(high - newer) + jnp.dot(
                    v_s[:, keys], expo, preferred_element_type=F32
                )
                result.append((newer, total))
            return tuple(result)

        carry = tuple(
            (jnp.full((1, QT), NEG, F32), jnp.zeros((VROWS, QT), F32)) for _ in range(SIDE)
        )
        carry = lax.fori_loop(0, big, functools.partial(one_chunk, KT, 0), carry)
        carry = lax.fori_loop(
            0, small, functools.partial(one_chunk, KT // 2, big * per_k), carry
        )
        for (t, _, _), (_, total) in zip(tiles, carry):
            o_s[:, pl.ds(pl.multiple_of(t * QT, QT), QT)] = total / total[HD : HD + 1, :]
        return 0

    lax.fori_loop(0, length // (QT * SIDE), some_tiles, 0)
    tok = length // n_seq
    for s in range(n_seq):
        mine = o_s[0:HD, s * tok : (s + 1) * tok]
        rest = mine[:, LANES:tok]
        out_ref[s, 0:64, :] = mine[0:64, 0:LANES].astype(BF)
        out_ref[s, 64:96, :] = jnp.concatenate([rest[0:32], rest[32:64]], axis=1).astype(BF)
        empty = jnp.zeros((HD - 64, 2 * LANES - tok), F32)
        out_ref[s, 96:112, :] = jnp.concatenate(
            [mine[64:HD, 0:LANES], jnp.concatenate([rest[64:HD], empty], axis=1)], axis=0
        ).astype(BF)


def project_kernel(n_seq, in_ref, w_ref, out_ref):
    width = out_ref.shape[1]
    tok = out_ref.shape[0]
    rest = tok - LANES
    lo = in_ref[:, 0:32, :].reshape(n_seq * 32, LANES)
    hi = in_ref[:, 32:64, :].reshape(n_seq * 32, LANES)
    far = in_ref[:, 64:96, :].reshape(n_seq * 32, LANES)
    tail = in_ref[:, 96:112, :].reshape(n_seq * 16, LANES).astype(F32)
    upper = (iota(tail.shape, 0) & 15) < 8
    tail_near = jnp.where(upper, tail, 0.0).astype(BF)
    tail_far = jnp.where(upper, 0.0, tail).astype(BF)
    near = jnp.concatenate([lo, hi, tail_near], axis=0).T
    far_t = far.T
    distant = jnp.concatenate([far_t[0:rest], far_t[rest:LANES], tail_far.T[0:rest]], axis=1)
    left = jnp.concatenate([near, distant], axis=0)
    last = w_ref[:, 64:HD, :].astype(F32)
    weights = jnp.concatenate(
        [
            w_ref[:, 0:32, :].reshape(n_seq * 32, width),
            w_ref[:, 32:64, :].reshape(n_seq * 32, width),
            jnp.concatenate([last, last], axis=1).reshape(n_seq * 16, width).astype(BF),
        ],
        axis=0,
    )
    out_ref[...] = jnp.dot(left, weights, preferred_element_type=F32).astype(BF)


def cost(flops, operands, out_shape):
    total = sum(math.prod(x.shape) * x.dtype.itemsize for x in operands)
    total += sum(math.prod(x.shape) * x.dtype.itemsize for x in jax.tree.leaves(out_shape))
    return pl.CostEstimate(flops=flops, bytes_accessed=total, transcendentals=0)


def local_call(kernel, out_shape, *operands, name, flops, small=0, scratch=(), behind=(), mib=30):
    smem = pl.BlockSpec(memory_space=pltpu.SMEM)
    vmem = pl.BlockSpec(memory_space=pltpu.VMEM)
    after = [pl.BlockSpec(memory_space=pl.ANY)] * len(behind)
    return pl.pallas_call(
        kernel,
        out_shape=out_shape,
        in_specs=[smem] * small + [vmem] * (len(operands) - small) + after,
        out_specs=jax.tree.map(lambda _: vmem, out_shape),
        scratch_shapes=scratch,
        compiler_params=pltpu.CompilerParams(vmem_limit_bytes=mib * 2**20),
        cost_estimate=cost(flops, operands, out_shape),
        name=name,
    )(*operands, *behind)


def project_qkv(blocks, mine_w, pair_w, name):
    rows = sum(x.shape[0] for x in blocks)
    out = jax.ShapeDtypeStruct((rows // TOK, TOK, QKV), BF)
    flops = 2 * rows * mine_w.shape[1] * 6 * HD
    return local_call(
        qkv_kernel, (out, out), *blocks, mine_w, pair_w, name=name, flops=flops
    )


def attend_call(me, doc_ids, n_seq, *blocks):
    length = n_seq * TOK
    return local_call(
        functools.partial(attend_kernel, n_seq),
        jax.ShapeDtypeStruct((n_seq, AROWS, LANES), BF),
        me,
        doc_ids,
        *blocks,
        small=2,
        flops=2 * length * length * HD,
        scratch=[
            pltpu.VMEM((length, HD), BF),
            pltpu.VMEM((length + KT, HD), BF),
            pltpu.VMEM((length, LANES), BF),
            pltpu.VMEM((VROWS, length + KT), BF),
            pltpu.VMEM((VROWS, length), F32),
            pltpu.SMEM((2, length // BLK), jnp.int32),
        ],
        name="attend",
    )


def halves_kernel(right_ref, left_ref, *refs):
    *_, top_ref, bottom_ref = refs
    half = top_ref.shape[0]
    top_ref[...] = right_ref[0:half, :]
    bottom_ref[...] = left_ref[half:, :]


def ring_step(right, left, n_seq):
    up = [(i, (i + 2) % n_seq) for i in range(n_seq)]
    down = [(i, (i - 2) % n_seq) for i in range(n_seq)]
    return lax.ppermute(right, "seq", up), lax.ppermute(left, "seq", down)


def body(source, destination, doc_ids, w_qkv, w_out):
    n_pack = lax.axis_size("pack")
    n_seq = lax.axis_size("seq")
    width = source.shape[2]
    shape = jax.ShapeDtypeStruct
    me = lax.axis_index("seq").astype(jnp.int32).reshape(1)
    w_t = jnp.transpose(w_qkv, (0, 2, 1)).reshape(3 * HD, width)

    def other_core(x):
        return lax.ppermute(x, "seq", [(i, i ^ 1) for i in range(n_seq)])

    outbox = local_call(
        functools.partial(pack_kernel, n_pack),
        shape((n_pack, TILES * 16, LANES), BF),
        destination,
        source[0],
        name="pack_rows",
        flops=10**9,
        mib=56,
    )
    inbox = lax.all_to_all(outbox, "pack", split_axis=0, concat_axis=0, tiled=True)

    pair_w = other_core(w_t)
    w_all = lax.all_gather(w_out, "seq", axis=0, tiled=False)

    packed = local_call(
        functools.partial(unpack_kernel, n_pack),
        shape((TOK, width), BF),
        inbox,
        name="unpack_rows",
        flops=10**9,
        behind=(pair_w,),
    )
    right = left = packed
    held = [packed]
    for _ in range(3):
        right, left = ring_step(right, left, n_seq)
        held += [right, left]
    mine, theirs = project_qkv(held[:5], w_t, pair_w, "qkv_first")
    half = shape((TOK // 2, width), BF)
    top, bottom = local_call(
        halves_kernel, (half, half), right, left, behind=(theirs,), name="halves", flops=0
    )
    held += ring_step(top, bottom, n_seq)
    last_mine, last_theirs = project_qkv(held[5:], w_t, pair_w, "qkv_last")
    ours = [mine, last_mine, other_core(theirs), other_core(last_theirs)]
    attended = attend_call(me, doc_ids, n_seq, *ours)
    blocks = lax.all_to_all(attended, "seq", split_axis=0, concat_axis=0, tiled=True)

    out = local_call(
        functools.partial(project_kernel, n_seq),
        shape((TOK, width), BF),
        blocks,
        w_all,
        name="project",
        flops=2 * TOK * width * width,
    )
    return out[None]


def solution(mesh):
    placed = (
        P("seq", "pack", None),
        P("seq", "pack"),
        P("pack", None),
        P(None, None, "seq"),
        P("seq", None),
    )
    return jax.shard_map(
        body, mesh=mesh, in_specs=placed, out_specs=P("pack", "seq", None), check_vma=False
    )
```

```python
import functools
import math

import jax
import jax.numpy as jnp
from jax import lax
from jax.experimental import pallas as pl
from jax.experimental.pallas import tpu as pltpu
from jax.sharding import PartitionSpec as P

HD = 72
CAP = 12
LANES = 128
BLK = 128
BF = jnp.bfloat16
F32 = jnp.float32
NT = (((1,), (1,)), ((), ()))

SHIFTS = (
    (0, ((0, 0), (3, 4), (6, 8))),
    (-12, ((0, 1), (3, 5))),
    (4, ((1, 1), (4, 5))),
    (-8, ((1, 2), (4, 6))),
    (8, ((2, 2), (5, 6))),
    (-4, ((2, 3), (5, 7))),
)
TILES = 7


def iota(shape, dim):
    return lax.broadcasted_iota(jnp.int32, shape, dim)


def onehot(condition):
    return jnp.where(condition, 1.0, 0.0).astype(BF)


def pack_kernel(n_pack, dest_ref, rows_ref, out_ref):
    tok = rows_ref.shape[0]
    group = n_pack * 16
    dest = dest_ref[...]
    owner = ((dest >> 6) * 171) >> 9
    place = dest - owner * tok
    owned = iota((n_pack, tok), 0) == owner
    before = onehot(iota((tok, tok), 0) < iota((tok, tok), 1))
    counted = jnp.dot(onehot(owned), before, preferred_element_type=F32)
    slot = jnp.sum(jnp.where(owned, counted, 0.0), axis=0, keepdims=True).astype(jnp.int32)
    row = iota((group, tok), 0)
    parts = {}
    for shift, pairs in SHIFTS:
        at = slot - shift
        key = jnp.where((at >= 0) & (at < 16), owner * 16 + at, -1)
        picked = jnp.concatenate(
            [rows_ref[:, f * LANES : (f + 1) * LANES] for _, f in pairs], axis=1
        )
        moved = jnp.dot(onehot(row == key), picked, preferred_element_type=F32)
        for n, (tile, _) in enumerate(pairs):
            parts.setdefault(tile, []).append(moved[:, n * LANES : (n + 1) * LANES])
    tags = jnp.where(iota((LANES, tok), 0) == slot, (place + 1).astype(F32), 0.0).astype(BF)
    here = onehot(row == owner * 16 + CAP)
    parts[TILES - 1].append(lax.dot_general(here, tags, NT, preferred_element_type=F32))
    for tile in range(TILES):
        whole = functools.reduce(lambda a, b: a + b, parts[tile])
        out_ref[:, tile * 16 : (tile + 1) * 16, :] = whole.astype(BF).reshape(n_pack, 16, LANES)


def unpack_kernel(n_pack, in_ref, *refs):
    out_ref = refs[-1]
    tok = out_ref.shape[0]
    group = n_pack * 16
    tiles = [in_ref[:, t * 16 : (t + 1) * 16, :].reshape(group, LANES) for t in range(TILES)]
    col = iota((n_pack, group), 1)
    lead = iota((n_pack, group), 0) * 16
    labels = jnp.dot(onehot(col == lead + CAP), tiles[-1], preferred_element_type=F32).astype(BF)
    mine = (col >= lead) & (col < lead + 16)
    offset = iota((LANES, group), 0) - (iota((LANES, group), 1) & 15)
    place = iota((tok, group), 0) + 1
    parts = {}
    for shift, pairs in SHIFTS:
        spread = jnp.dot(labels, onehot(offset == shift), preferred_element_type=F32)
        label = jnp.sum(jnp.where(mine, spread, 0.0), axis=0, keepdims=True).astype(jnp.int32)
        picked = jnp.concatenate([tiles[t] for t, _ in pairs], axis=1)
        moved = jnp.dot(onehot(place == label), picked, preferred_element_type=F32)
        for n, (_, f) in enumerate(pairs):
            parts.setdefault(f, []).append(moved[:, n * LANES : (n + 1) * LANES])
    for f in sorted(parts):
        whole = functools.reduce(lambda a, b: a + b, parts[f])
        out_ref[:, f * LANES : (f + 1) * LANES] = whole.astype(BF)


TOK = 192
QT = 768
KT = 1024
SIDE = 1
VROWS = 80
QKV = 256
AROWS = 112
NEG = -3e38
BACK = (0, 1, -1, 2, -2, 3, -3, 4)


def origin(me, n):
    chips = len(BACK)
    core = me & 1
    chip = ((me >> 1) - BACK[n % chips]) & (chips - 1)
    return 2 * chip + (core if n < chips else 1 - core)


def qkv_kernel(*refs):
    *x_refs, mine_w_ref, pair_w_ref, mine_ref, pair_ref = refs
    x = jnp.concatenate([ref[...] for ref in x_refs], axis=0)
    rows = x.shape[0]
    scale = jnp.where(iota((1, 3 * HD), 1) < HD, math.log2(math.e) / math.sqrt(HD), 1.0)
    fill = jnp.where(iota((rows, QKV - 3 * HD), 1) < VROWS - HD, 1.0, 0.0)
    for w_ref, out_ref in ((mine_w_ref, mine_ref), (pair_w_ref, pair_ref)):
        qkv = lax.dot_general(x, w_ref[...], NT, preferred_element_type=F32) * scale
        whole = jnp.concatenate([qkv, fill], axis=1).astype(BF)
        out_ref[...] = whole.reshape(rows // TOK, TOK, QKV)


def attend_kernel(n_seq, me_ref, doc_ref, *refs):
    *in_refs, out_ref, q_s, k_s, row_s, v_s, o_s, bound_s = refs
    n = 0
    for ref in in_refs:
        for i in range(ref.shape[0]):
            rows = pl.ds(pl.multiple_of(origin(me_ref[0], n) * TOK, 64), TOK)
            q_s[rows, :] = ref[i, :, 0:HD]
            k_s[rows, :] = ref[i, :, HD : 2 * HD]
            row_s[rows, :] = ref[i, :, LANES:QKV]
            n += 1
    length = q_s.shape[0]
    blocks = length // BLK
    per_q = QT // BLK
    per_k = KT // BLK
    for b in range(blocks):
        turned = row_s[b * BLK : (b + 1) * BLK, :].T
        begin = 2 * HD - LANES
        v_s[:, b * BLK : (b + 1) * BLK] = turned[begin : begin + VROWS, :]
    k_s[length:, :] = jnp.zeros((KT, HD), BF)
    v_s[:, length:] = jnp.zeros((VROWS, KT), BF)
    first = jnp.int32(0)
    for b in range(blocks):
        if b:
            first = jnp.where(doc_ref[0, b * BLK] == doc_ref[0, (b - 1) * BLK], first, b)
        bound_s[0, b] = first
    last = jnp.int32(blocks)
    for b in reversed(range(blocks)):
        if b < blocks - 1:
            last = jnp.where(doc_ref[0, b * BLK] == doc_ref[0, (b + 1) * BLK], last, b + 1)
        bound_s[1, b] = last

    def some_tiles(group, _):
        tiles = []
        for u in range(SIDE):
            t = group * SIDE + u
            bounds = [
                (bound_s[0, t * per_q + i], bound_s[1, t * per_q + i]) for i in range(per_q)
            ]
            q = q_s[pl.ds(pl.multiple_of(t * QT, QT), QT), :]
            tiles.append((t, q, bounds))
        chunks = functools.reduce(
            jnp.maximum, [b[-1][1] - b[0][0] for _, _, b in tiles]
        )
        big = (chunks + per_k // 2 - 1) // per_k
        small = jnp.where(chunks > big * per_k, 1, 0)

        def one_chunk(width, base, c, carry):
            result = []
            for (_, q, bounds), (high, total) in zip(tiles, carry):
                begin = bounds[0][0] + base + c * (width // BLK)
                keys = pl.ds(pl.multiple_of(jnp.minimum(begin, blocks) * BLK, BLK), width)
                scores = lax.dot_general(k_s[keys, :], q, NT, preferred_element_type=F32)
                columns = []
                for i, (lo, hi) in enumerate(bounds):
                    kept = [
                        jnp.where(
                            (begin + j >= lo) & (begin + j < hi),
                            scores[j * BLK : (j + 1) * BLK, i * BLK : (i + 1) * BLK],
                            -jnp.inf,
                        )
                        for j in range(width // BLK)
                    ]
                    columns.append(jnp.concatenate(kept, axis=0))
                scores = jnp.concatenate(columns, axis=1)
                newer = jnp.maximum(high, jnp.max(scores, axis=0, keepdims=True))
                expo = jnp.exp2(scores - newer).astype(BF)
                total = total * jnp.exp2(high - newer) + jnp.dot(
                    v_s[:, keys], expo, preferred_element_type=F32
                )
                result.append((newer, total))
            return tuple(result)

        carry = tuple(
            (jnp.full((1, QT), NEG, F32), jnp.zeros((VROWS, QT), F32)) for _ in range(SIDE)
        )
        carry = lax.fori_loop(0, big, functools.partial(one_chunk, KT, 0), carry)
        carry = lax.fori_loop(
            0, small, functools.partial(one_chunk, KT // 2, big * per_k), carry
        )
        for (t, _, _), (_, total) in zip(tiles, carry):
            o_s[:, pl.ds(pl.multiple_of(t * QT, QT), QT)] = total / total[HD : HD + 1, :]
        return 0

    lax.fori_loop(0, length // (QT * SIDE), some_tiles, 0)
    tok = length // n_seq
    for s in range(n_seq):
        mine = o_s[0:HD, s * tok : (s + 1) * tok]
        rest = mine[:, LANES:tok]
        out_ref[s, 0:64, :] = mine[0:64, 0:LANES].astype(BF)
        out_ref[s, 64:96, :] = jnp.concatenate([rest[0:32], rest[32:64]], axis=1).astype(BF)
        empty = jnp.zeros((HD - 64, 2 * LANES - tok), F32)
        out_ref[s, 96:112, :] = jnp.concatenate(
            [mine[64:HD, 0:LANES], jnp.concatenate([rest[64:HD], empty], axis=1)], axis=0
        ).astype(BF)


def project_kernel(n_seq, in_ref, w_ref, out_ref):
    width = out_ref.shape[1]
    tok = out_ref.shape[0]
    rest = tok - LANES
    lo = in_ref[:, 0:32, :].reshape(n_seq * 32, LANES)
    hi = in_ref[:, 32:64, :].reshape(n_seq * 32, LANES)
    far = in_ref[:, 64:96, :].reshape(n_seq * 32, LANES)
    tail = in_ref[:, 96:112, :].reshape(n_seq * 16, LANES).astype(F32)
    upper = (iota(tail.shape, 0) & 15) < 8
    tail_near = jnp.where(upper, tail, 0.0).astype(BF)
    tail_far = jnp.where(upper, 0.0, tail).astype(BF)
    near = jnp.concatenate([lo, hi, tail_near], axis=0).T
    far_t = far.T
    distant = jnp.concatenate([far_t[0:rest], far_t[rest:LANES], tail_far.T[0:rest]], axis=1)
    left = jnp.concatenate([near, distant], axis=0)
    last = w_ref[:, 64:HD, :].astype(F32)
    weights = jnp.concatenate(
        [
            w_ref[:, 0:32, :].reshape(n_seq * 32, width),
            w_ref[:, 32:64, :].reshape(n_seq * 32, width),
            jnp.concatenate([last, last], axis=1).reshape(n_seq * 16, width).astype(BF),
        ],
        axis=0,
    )
    out_ref[...] = jnp.dot(left, weights, preferred_element_type=F32).astype(BF)


def cost(flops, operands, out_shape):
    total = sum(math.prod(x.shape) * x.dtype.itemsize for x in operands)
    total += sum(math.prod(x.shape) * x.dtype.itemsize for x in jax.tree.leaves(out_shape))
    return pl.CostEstimate(flops=flops, bytes_accessed=total, transcendentals=0)


def local_call(kernel, out_shape, *operands, name, flops, small=0, scratch=(), behind=(), mib=30):
    smem = pl.BlockSpec(memory_space=pltpu.SMEM)
    vmem = pl.BlockSpec(memory_space=pltpu.VMEM)
    after = [pl.BlockSpec(memory_space=pl.ANY)] * len(behind)
    return pl.pallas_call(
        kernel,
        out_shape=out_shape,
        in_specs=[smem] * small + [vmem] * (len(operands) - small) + after,
        out_specs=jax.tree.map(lambda _: vmem, out_shape),
        scratch_shapes=scratch,
        compiler_params=pltpu.CompilerParams(vmem_limit_bytes=mib * 2**20),
        cost_estimate=cost(flops, operands, out_shape),
        name=name,
    )(*operands, *behind)


def project_qkv(blocks, mine_w, pair_w, name):
    rows = sum(x.shape[0] for x in blocks)
    out = jax.ShapeDtypeStruct((rows // TOK, TOK, QKV), BF)
    flops = 2 * rows * mine_w.shape[1] * 6 * HD
    return local_call(
        qkv_kernel, (out, out), *blocks, mine_w, pair_w, name=name, flops=flops
    )


def attend_call(me, doc_ids, n_seq, *blocks):
    length = n_seq * TOK
    return local_call(
        functools.partial(attend_kernel, n_seq),
        jax.ShapeDtypeStruct((n_seq, AROWS, LANES), BF),
        me,
        doc_ids,
        *blocks,
        small=2,
        flops=2 * length * length * HD,
        scratch=[
            pltpu.VMEM((length, HD), BF),
            pltpu.VMEM((length + KT, HD), BF),
            pltpu.VMEM((length, LANES), BF),
            pltpu.VMEM((VROWS, length + KT), BF),
            pltpu.VMEM((VROWS, length), F32),
            pltpu.SMEM((2, length // BLK), jnp.int32),
        ],
        name="attend",
    )


def pick_kernel(me_ref, right_ref, left_ref, *refs):
    out_ref = refs[-1]

    @pl.when((me_ref[0] & 1) == 0)
    def _():
        out_ref[...] = right_ref[...]

    @pl.when((me_ref[0] & 1) == 1)
    def _():
        out_ref[...] = left_ref[...]


def ring_step(right, left, n_seq):
    up = [(i, (i + 2) % n_seq) for i in range(n_seq)]
    down = [(i, (i - 2) % n_seq) for i in range(n_seq)]
    return lax.ppermute(right, "seq", up), lax.ppermute(left, "seq", down)


def body(source, destination, doc_ids, w_qkv, w_out):
    n_pack = lax.axis_size("pack")
    n_seq = lax.axis_size("seq")
    width = source.shape[2]
    shape = jax.ShapeDtypeStruct
    me = lax.axis_index("seq").astype(jnp.int32).reshape(1)
    w_t = jnp.transpose(w_qkv, (0, 2, 1)).reshape(3 * HD, width)

    def other_core(x):
        return lax.ppermute(x, "seq", [(i, i ^ 1) for i in range(n_seq)])

    outbox = local_call(
        functools.partial(pack_kernel, n_pack),
        shape((n_pack, TILES * 16, LANES), BF),
        destination,
        source[0],
        name="pack_rows",
        flops=10**9,
        mib=56,
    )
    inbox = lax.all_to_all(outbox, "pack", split_axis=0, concat_axis=0, tiled=True)

    pair_w = other_core(w_t)
    w_all = lax.all_gather(w_out, "seq", axis=0, tiled=False)

    packed = local_call(
        functools.partial(unpack_kernel, n_pack),
        shape((TOK, width), BF),
        inbox,
        name="unpack_rows",
        flops=10**9,
        behind=(pair_w,),
    )
    right = left = packed
    held = [packed]
    for _ in range(3):
        right, left = ring_step(right, left, n_seq)
        held += [right, left]
    mine, theirs = project_qkv(held[:5], w_t, pair_w, "qkv_first")
    picked = local_call(
        pick_kernel,
        shape((TOK, width), BF),
        me,
        right,
        left,
        small=1,
        behind=(theirs,),
        name="pick",
        flops=0,
    )
    ways = [(i, (i + 2 - 4 * (i % 2)) % n_seq) for i in range(n_seq)]
    held.append(lax.ppermute(picked, "seq", ways))
    last_mine, last_theirs = project_qkv(held[5:], w_t, pair_w, "qkv_last")
    ours = [mine, last_mine, other_core(theirs), other_core(last_theirs)]
    attended = attend_call(me, doc_ids, n_seq, *ours)
    blocks = lax.all_to_all(attended, "seq", split_axis=0, concat_axis=0, tiled=True)

    out = local_call(
        functools.partial(project_kernel, n_seq),
        shape((TOK, width), BF),
        blocks,
        w_all,
        name="project",
        flops=2 * TOK * width * width,
    )
    return out[None]


def solution(mesh):
    placed = (
        P("seq", "pack", None),
        P("seq", "pack"),
        P("pack", None),
        P(None, None, "seq"),
        P("seq", None),
    )
    return jax.shard_map(
        body, mesh=mesh, in_specs=placed, out_specs=P("pack", "seq", None), check_vma=False
    )
```

```python
import functools
import math

import jax
import jax.numpy as jnp
from jax import lax
from jax.experimental import pallas as pl
from jax.experimental.pallas import tpu as pltpu
from jax.sharding import PartitionSpec as P

HD = 72
CAP = 12
LANES = 128
BLK = 128
BF = jnp.bfloat16
F32 = jnp.float32
NT = (((1,), (1,)), ((), ()))

SHIFTS = (
    (0, ((0, 0), (3, 4), (6, 8))),
    (-12, ((0, 1), (3, 5))),
    (4, ((1, 1), (4, 5))),
    (-8, ((1, 2), (4, 6))),
    (8, ((2, 2), (5, 6))),
    (-4, ((2, 3), (5, 7))),
)
TILES = 7


def iota(shape, dim):
    return lax.broadcasted_iota(jnp.int32, shape, dim)


def onehot(condition):
    return jnp.where(condition, 1.0, 0.0).astype(BF)


def pack_kernel(n_pack, dest_ref, rows_ref, out_ref):
    tok = rows_ref.shape[0]
    group = n_pack * 16
    dest = dest_ref[...]
    owner = ((dest >> 6) * 171) >> 9
    place = dest - owner * tok
    owned = iota((n_pack, tok), 0) == owner
    before = onehot(iota((tok, tok), 0) < iota((tok, tok), 1))
    counted = jnp.dot(onehot(owned), before, preferred_element_type=F32)
    slot = jnp.sum(jnp.where(owned, counted, 0.0), axis=0, keepdims=True).astype(jnp.int32)
    row = iota((group, tok), 0)
    parts = {}
    for shift, pairs in SHIFTS:
        at = slot - shift
        key = jnp.where((at >= 0) & (at < 16), owner * 16 + at, -1)
        picked = jnp.concatenate(
            [rows_ref[:, f * LANES : (f + 1) * LANES] for _, f in pairs], axis=1
        )
        moved = jnp.dot(onehot(row == key), picked, preferred_element_type=F32)
        for n, (tile, _) in enumerate(pairs):
            parts.setdefault(tile, []).append(moved[:, n * LANES : (n + 1) * LANES])
    tags = jnp.where(iota((LANES, tok), 0) == slot, (place + 1).astype(F32), 0.0).astype(BF)
    here = onehot(row == owner * 16 + CAP)
    parts[TILES - 1].append(lax.dot_general(here, tags, NT, preferred_element_type=F32))
    for tile in range(TILES):
        whole = functools.reduce(lambda a, b: a + b, parts[tile])
        out_ref[:, tile * 16 : (tile + 1) * 16, :] = whole.astype(BF).reshape(n_pack, 16, LANES)


def unpack_kernel(n_pack, in_ref, *refs):
    out_ref = refs[-1]
    tok = out_ref.shape[0]
    group = n_pack * 16
    tiles = [in_ref[:, t * 16 : (t + 1) * 16, :].reshape(group, LANES) for t in range(TILES)]
    col = iota((n_pack, group), 1)
    lead = iota((n_pack, group), 0) * 16
    labels = jnp.dot(onehot(col == lead + CAP), tiles[-1], preferred_element_type=F32).astype(BF)
    mine = (col >= lead) & (col < lead + 16)
    offset = iota((LANES, group), 0) - (iota((LANES, group), 1) & 15)
    place = iota((tok, group), 0) + 1
    parts = {}
    for shift, pairs in SHIFTS:
        spread = jnp.dot(labels, onehot(offset == shift), preferred_element_type=F32)
        label = jnp.sum(jnp.where(mine, spread, 0.0), axis=0, keepdims=True).astype(jnp.int32)
        picked = jnp.concatenate([tiles[t] for t, _ in pairs], axis=1)
        moved = jnp.dot(onehot(place == label), picked, preferred_element_type=F32)
        for n, (_, f) in enumerate(pairs):
            parts.setdefault(f, []).append(moved[:, n * LANES : (n + 1) * LANES])
    for f in sorted(parts):
        whole = functools.reduce(lambda a, b: a + b, parts[f])
        out_ref[:, f * LANES : (f + 1) * LANES] = whole.astype(BF)


TOK = 192
QT = 768
KT = 1024
SIDE = 1
VROWS = 80
QKV = 256
AROWS = 112
NEG = -3e38
BACK = (0, 1, -1, 2, -2, 3, -3, 4)


def origin(me, n):
    chips = len(BACK)
    core = me & 1
    chip = ((me >> 1) - BACK[n % chips]) & (chips - 1)
    return 2 * chip + (core if n < chips else 1 - core)


def qkv_kernel(*refs):
    *x_refs, mine_w_ref, pair_w_ref, mine_ref, pair_ref = refs
    x = jnp.concatenate([ref[...] for ref in x_refs], axis=0)
    rows = x.shape[0]
    scale = jnp.where(iota((1, 3 * HD), 1) < HD, math.log2(math.e) / math.sqrt(HD), 1.0)
    fill = jnp.where(iota((rows, QKV - 3 * HD), 1) < VROWS - HD, 1.0, 0.0)
    for w_ref, out_ref in ((mine_w_ref, mine_ref), (pair_w_ref, pair_ref)):
        qkv = lax.dot_general(x, w_ref[...], NT, preferred_element_type=F32) * scale
        whole = jnp.concatenate([qkv, fill], axis=1).astype(BF)
        out_ref[...] = whole.reshape(rows // TOK, TOK, QKV)


def attend_kernel(n_seq, me_ref, doc_ref, *refs):
    *in_refs, out_ref, q_s, k_s, row_s, v_s, o_s, bound_s = refs
    n = 0
    for ref in in_refs:
        for i in range(ref.shape[0]):
            rows = pl.ds(pl.multiple_of(origin(me_ref[0], n) * TOK, 64), TOK)
            q_s[rows, :] = ref[i, :, 0:HD]
            k_s[rows, :] = ref[i, :, HD : 2 * HD]
            row_s[rows, :] = ref[i, :, LANES:QKV]
            n += 1
    length = q_s.shape[0]
    blocks = length // BLK
    per_q = QT // BLK
    per_k = KT // BLK
    for b in range(blocks):
        turned = row_s[b * BLK : (b + 1) * BLK, :].T
        begin = 2 * HD - LANES
        v_s[:, b * BLK : (b + 1) * BLK] = turned[begin : begin + VROWS, :]
    k_s[length:, :] = jnp.zeros((KT, HD), BF)
    v_s[:, length:] = jnp.zeros((VROWS, KT), BF)
    first = jnp.int32(0)
    for b in range(blocks):
        if b:
            first = jnp.where(doc_ref[0, b * BLK] == doc_ref[0, (b - 1) * BLK], first, b)
        bound_s[0, b] = first
    last = jnp.int32(blocks)
    for b in reversed(range(blocks)):
        if b < blocks - 1:
            last = jnp.where(doc_ref[0, b * BLK] == doc_ref[0, (b + 1) * BLK], last, b + 1)
        bound_s[1, b] = last

    def some_tiles(group, _):
        tiles = []
        for u in range(SIDE):
            t = group * SIDE + u
            bounds = [
                (bound_s[0, t * per_q + i], bound_s[1, t * per_q + i]) for i in range(per_q)
            ]
            q = q_s[pl.ds(pl.multiple_of(t * QT, QT), QT), :]
            tiles.append((t, q, bounds))
        chunks = functools.reduce(
            jnp.maximum, [b[-1][1] - b[0][0] for _, _, b in tiles]
        )
        big = (chunks + per_k // 2 - 1) // per_k
        small = jnp.where(chunks > big * per_k, 1, 0)

        def one_chunk(width, base, c, carry):
            result = []
            for (_, q, bounds), (high, total) in zip(tiles, carry):
                begin = bounds[0][0] + base + c * (width // BLK)
                keys = pl.ds(pl.multiple_of(jnp.minimum(begin, blocks) * BLK, BLK), width)
                scores = lax.dot_general(k_s[keys, :], q, NT, preferred_element_type=F32)
                columns = []
                for i, (lo, hi) in enumerate(bounds):
                    kept = [
                        jnp.where(
                            (begin + j >= lo) & (begin + j < hi),
                            scores[j * BLK : (j + 1) * BLK, i * BLK : (i + 1) * BLK],
                            -jnp.inf,
                        )
                        for j in range(width // BLK)
                    ]
                    columns.append(jnp.concatenate(kept, axis=0))
                scores = jnp.concatenate(columns, axis=1)
                newer = jnp.maximum(high, jnp.max(scores, axis=0, keepdims=True))
                expo = jnp.exp2(scores - newer).astype(BF)
                total = total * jnp.exp2(high - newer) + jnp.dot(
                    v_s[:, keys], expo, preferred_element_type=F32
                )
                result.append((newer, total))
            return tuple(result)

        carry = tuple(
            (jnp.full((1, QT), NEG, F32), jnp.zeros((VROWS, QT), F32)) for _ in range(SIDE)
        )
        carry = lax.fori_loop(0, big, functools.partial(one_chunk, KT, 0), carry)
        carry = lax.fori_loop(
            0, small, functools.partial(one_chunk, KT // 2, big * per_k), carry
        )
        for (t, _, _), (_, total) in zip(tiles, carry):
            o_s[:, pl.ds(pl.multiple_of(t * QT, QT), QT)] = total / total[HD : HD + 1, :]
        return 0

    lax.fori_loop(0, length // (QT * SIDE), some_tiles, 0)
    tok = length // n_seq
    for s in range(n_seq):
        mine = o_s[0:HD, s * tok : (s + 1) * tok]
        rest = mine[:, LANES:tok]
        out_ref[s, 0:64, :] = mine[0:64, 0:LANES].astype(BF)
        out_ref[s, 64:96, :] = jnp.concatenate([rest[0:32], rest[32:64]], axis=1).astype(BF)
        empty = jnp.zeros((HD - 64, 2 * LANES - tok), F32)
        out_ref[s, 96:112, :] = jnp.concatenate(
            [mine[64:HD, 0:LANES], jnp.concatenate([rest[64:HD], empty], axis=1)], axis=0
        ).astype(BF)


def project_kernel(n_seq, in_ref, w_ref, out_ref):
    width = out_ref.shape[1]
    tok = out_ref.shape[0]
    rest = tok - LANES
    lo = in_ref[:, 0:32, :].reshape(n_seq * 32, LANES)
    hi = in_ref[:, 32:64, :].reshape(n_seq * 32, LANES)
    far = in_ref[:, 64:96, :].reshape(n_seq * 32, LANES)
    tail = in_ref[:, 96:112, :].reshape(n_seq * 16, LANES).astype(F32)
    upper = (iota(tail.shape, 0) & 15) < 8
    tail_near = jnp.where(upper, tail, 0.0).astype(BF)
    tail_far = jnp.where(upper, 0.0, tail).astype(BF)
    near = jnp.concatenate([lo, hi, tail_near], axis=0).T
    far_t = far.T
    distant = jnp.concatenate([far_t[0:rest], far_t[rest:LANES], tail_far.T[0:rest]], axis=1)
    left = jnp.concatenate([near, distant], axis=0)
    last = w_ref[:, 64:HD, :].astype(F32)
    weights = jnp.concatenate(
        [
            w_ref[:, 0:32, :].reshape(n_seq * 32, width),
            w_ref[:, 32:64, :].reshape(n_seq * 32, width),
            jnp.concatenate([last, last], axis=1).reshape(n_seq * 16, width).astype(BF),
        ],
        axis=0,
    )
    out_ref[...] = jnp.dot(left, weights, preferred_element_type=F32).astype(BF)


def cost(flops, operands, out_shape):
    total = sum(math.prod(x.shape) * x.dtype.itemsize for x in operands)
    total += sum(math.prod(x.shape) * x.dtype.itemsize for x in jax.tree.leaves(out_shape))
    return pl.CostEstimate(flops=flops, bytes_accessed=total, transcendentals=0)


def local_call(kernel, out_shape, *operands, name, flops, small=0, scratch=(), behind=(), mib=30):
    smem = pl.BlockSpec(memory_space=pltpu.SMEM)
    vmem = pl.BlockSpec(memory_space=pltpu.VMEM)
    after = [pl.BlockSpec(memory_space=pl.ANY)] * len(behind)
    return pl.pallas_call(
        kernel,
        out_shape=out_shape,
        in_specs=[smem] * small + [vmem] * (len(operands) - small) + after,
        out_specs=jax.tree.map(lambda _: vmem, out_shape),
        scratch_shapes=scratch,
        compiler_params=pltpu.CompilerParams(vmem_limit_bytes=mib * 2**20),
        cost_estimate=cost(flops, operands, out_shape),
        name=name,
    )(*operands, *behind)


def project_qkv(blocks, mine_w, pair_w, name):
    rows = sum(x.shape[0] for x in blocks)
    out = jax.ShapeDtypeStruct((rows // TOK, TOK, QKV), BF)
    flops = 2 * rows * mine_w.shape[1] * 6 * HD
    return local_call(
        qkv_kernel, (out, out), *blocks, mine_w, pair_w, name=name, flops=flops
    )


def attend_call(me, doc_ids, n_seq, *blocks):
    length = n_seq * TOK
    return local_call(
        functools.partial(attend_kernel, n_seq),
        jax.ShapeDtypeStruct((n_seq, AROWS, LANES), BF),
        me,
        doc_ids,
        *blocks,
        small=2,
        flops=2 * length * length * HD,
        scratch=[
            pltpu.VMEM((length, HD), BF),
            pltpu.VMEM((length + KT, HD), BF),
            pltpu.VMEM((length, LANES), BF),
            pltpu.VMEM((VROWS, length + KT), BF),
            pltpu.VMEM((VROWS, length), F32),
            pltpu.SMEM((2, length // BLK), jnp.int32),
        ],
        name="attend",
    )


def pick_kernel(me_ref, right_ref, left_ref, *refs):
    out_ref = refs[-1]

    @pl.when((me_ref[0] & 1) == 0)
    def _():
        out_ref[...] = right_ref[...]

    @pl.when((me_ref[0] & 1) == 1)
    def _():
        out_ref[...] = left_ref[...]


def ring_step(right, left, n_seq):
    up = [(i, (i + 2) % n_seq) for i in range(n_seq)]
    down = [(i, (i - 2) % n_seq) for i in range(n_seq)]
    return lax.ppermute(right, "seq", up), lax.ppermute(left, "seq", down)


def body(source, destination, doc_ids, w_qkv, w_out):
    n_pack = lax.axis_size("pack")
    n_seq = lax.axis_size("seq")
    width = source.shape[2]
    shape = jax.ShapeDtypeStruct
    me = lax.axis_index("seq").astype(jnp.int32).reshape(1)
    w_t = jnp.transpose(w_qkv, (0, 2, 1)).reshape(3 * HD, width)

    def other_core(x):
        return lax.ppermute(x, "seq", [(i, i ^ 1) for i in range(n_seq)])

    outbox = local_call(
        functools.partial(pack_kernel, n_pack),
        shape((n_pack, TILES * 16, LANES), BF),
        destination,
        source[0],
        name="pack_rows",
        flops=10**9,
        mib=56,
    )
    inbox = lax.all_to_all(outbox, "pack", split_axis=0, concat_axis=0, tiled=True)

    pair_w = other_core(w_t)
    w_all = lax.all_gather(w_out, "seq", axis=0, tiled=False)

    packed = local_call(
        functools.partial(unpack_kernel, n_pack),
        shape((TOK, width), BF),
        inbox,
        name="unpack_rows",
        flops=10**9,
        behind=(pair_w,),
    )
    right = left = packed
    held = [packed]
    for _ in range(3):
        right, left = ring_step(right, left, n_seq)
        held += [right, left]
    mine, theirs = project_qkv(held[:5], w_t, pair_w, "qkv_first")
    picked = local_call(
        pick_kernel,
        shape((TOK, width), BF),
        me,
        right,
        left,
        small=1,
        behind=(theirs, w_all[0, 0:16, 0:LANES]),
        name="pick",
        flops=0,
    )
    ways = [(i, (i + 2 - 4 * (i % 2)) % n_seq) for i in range(n_seq)]
    held.append(lax.ppermute(picked, "seq", ways))
    last_mine, last_theirs = project_qkv(held[5:], w_t, pair_w, "qkv_last")
    ours = [mine, last_mine, other_core(theirs), other_core(last_theirs)]
    attended = attend_call(me, doc_ids, n_seq, *ours)
    blocks = lax.all_to_all(attended, "seq", split_axis=0, concat_axis=0, tiled=True)

    out = local_call(
        functools.partial(project_kernel, n_seq),
        shape((TOK, width), BF),
        blocks,
        w_all,
        name="project",
        flops=2 * TOK * width * width,
    )
    return out[None]


def solution(mesh):
    placed = (
        P("seq", "pack", None),
        P("seq", "pack"),
        P("pack", None),
        P(None, None, "seq"),
        P("seq", None),
    )
    return jax.shard_map(
        body, mesh=mesh, in_specs=placed, out_specs=P("pack", "seq", None), check_vma=False
    )
```

```python
import functools
import math

import jax
import jax.numpy as jnp
from jax import lax
from jax.experimental import pallas as pl
from jax.experimental.pallas import tpu as pltpu
from jax.sharding import PartitionSpec as P

HD = 72
CAP = 12
LANES = 128
BLK = 128
BF = jnp.bfloat16
F32 = jnp.float32
NT = (((1,), (1,)), ((), ()))

SHIFTS = (
    (0, ((0, 0), (3, 4), (6, 8))),
    (-12, ((0, 1), (3, 5))),
    (4, ((1, 1), (4, 5))),
    (-8, ((1, 2), (4, 6))),
    (8, ((2, 2), (5, 6))),
    (-4, ((2, 3), (5, 7))),
)
TILES = 7


def iota(shape, dim):
    return lax.broadcasted_iota(jnp.int32, shape, dim)


def onehot(condition):
    return jnp.where(condition, 1.0, 0.0).astype(BF)


def pack_kernel(n_pack, dest_ref, rows_ref, out_ref):
    tok = rows_ref.shape[0]
    group = n_pack * 16
    dest = dest_ref[...]
    owner = ((dest >> 6) * 171) >> 9
    place = dest - owner * tok
    owned = iota((n_pack, tok), 0) == owner
    before = onehot(iota((tok, tok), 0) < iota((tok, tok), 1))
    counted = jnp.dot(onehot(owned), before, preferred_element_type=F32)
    slot = jnp.sum(jnp.where(owned, counted, 0.0), axis=0, keepdims=True).astype(jnp.int32)
    row = iota((group, tok), 0)
    parts = {}
    for shift, pairs in SHIFTS:
        at = slot - shift
        key = jnp.where((at >= 0) & (at < 16), owner * 16 + at, -1)
        picked = jnp.concatenate(
            [rows_ref[:, f * LANES : (f + 1) * LANES] for _, f in pairs], axis=1
        )
        moved = jnp.dot(onehot(row == key), picked, preferred_element_type=F32)
        for n, (tile, _) in enumerate(pairs):
            parts.setdefault(tile, []).append(moved[:, n * LANES : (n + 1) * LANES])
    tags = jnp.where(iota((LANES, tok), 0) == slot, (place + 1).astype(F32), 0.0).astype(BF)
    here = onehot(row == owner * 16 + CAP)
    parts[TILES - 1].append(lax.dot_general(here, tags, NT, preferred_element_type=F32))
    for tile in range(TILES):
        whole = functools.reduce(lambda a, b: a + b, parts[tile])
        out_ref[:, tile * 16 : (tile + 1) * 16, :] = whole.astype(BF).reshape(n_pack, 16, LANES)


def unpack_kernel(n_pack, in_ref, *refs):
    out_ref = refs[-1]
    tok = out_ref.shape[0]
    group = n_pack * 16
    tiles = [in_ref[:, t * 16 : (t + 1) * 16, :].reshape(group, LANES) for t in range(TILES)]
    col = iota((n_pack, group), 1)
    lead = iota((n_pack, group), 0) * 16
    labels = jnp.dot(onehot(col == lead + CAP), tiles[-1], preferred_element_type=F32).astype(BF)
    mine = (col >= lead) & (col < lead + 16)
    offset = iota((LANES, group), 0) - (iota((LANES, group), 1) & 15)
    place = iota((tok, group), 0) + 1
    parts = {}
    for shift, pairs in SHIFTS:
        spread = jnp.dot(labels, onehot(offset == shift), preferred_element_type=F32)
        label = jnp.sum(jnp.where(mine, spread, 0.0), axis=0, keepdims=True).astype(jnp.int32)
        picked = jnp.concatenate([tiles[t] for t, _ in pairs], axis=1)
        moved = jnp.dot(onehot(place == label), picked, preferred_element_type=F32)
        for n, (_, f) in enumerate(pairs):
            parts.setdefault(f, []).append(moved[:, n * LANES : (n + 1) * LANES])
    for f in sorted(parts):
        whole = functools.reduce(lambda a, b: a + b, parts[f])
        out_ref[:, f * LANES : (f + 1) * LANES] = whole.astype(BF)


TOK = 192
QT = 768
KT = 1024
SIDE = 1
VROWS = 80
QKV = 256
AROWS = 112
NEG = -3e38
BACK = (0, 1, -1, 2, -2, 3, -3, 4)


def origin(me, n):
    chips = len(BACK)
    core = me & 1
    chip = ((me >> 1) - BACK[n % chips]) & (chips - 1)
    return 2 * chip + (core if n < chips else 1 - core)


def qkv_kernel(count, *refs):
    x_refs = refs[:count]
    mine_w_ref, pair_w_ref = refs[count : count + 2]
    mine_ref, pair_ref = refs[-2:]
    x = jnp.concatenate([ref[...] for ref in x_refs], axis=0)
    rows = x.shape[0]
    scale = jnp.where(iota((1, 3 * HD), 1) < HD, math.log2(math.e) / math.sqrt(HD), 1.0)
    fill = jnp.where(iota((rows, QKV - 3 * HD), 1) < VROWS - HD, 1.0, 0.0)
    for w_ref, out_ref in ((mine_w_ref, mine_ref), (pair_w_ref, pair_ref)):
        qkv = lax.dot_general(x, w_ref[...], NT, preferred_element_type=F32) * scale
        whole = jnp.concatenate([qkv, fill], axis=1).astype(BF)
        out_ref[...] = whole.reshape(rows // TOK, TOK, QKV)


def attend_kernel(n_seq, me_ref, doc_ref, *refs):
    *in_refs, out_ref, q_s, k_s, row_s, v_s, o_s, bound_s = refs
    n = 0
    for ref in in_refs:
        for i in range(ref.shape[0]):
            rows = pl.ds(pl.multiple_of(origin(me_ref[0], n) * TOK, 64), TOK)
            q_s[rows, :] = ref[i, :, 0:HD]
            k_s[rows, :] = ref[i, :, HD : 2 * HD]
            row_s[rows, :] = ref[i, :, LANES:QKV]
            n += 1
    length = q_s.shape[0]
    blocks = length // BLK
    per_q = QT // BLK
    per_k = KT // BLK
    for b in range(blocks):
        turned = row_s[b * BLK : (b + 1) * BLK, :].T
        begin = 2 * HD - LANES
        v_s[:, b * BLK : (b + 1) * BLK] = turned[begin : begin + VROWS, :]
    k_s[length:, :] = jnp.zeros((KT, HD), BF)
    v_s[:, length:] = jnp.zeros((VROWS, KT), BF)
    first = jnp.int32(0)
    for b in range(blocks):
        if b:
            first = jnp.where(doc_ref[0, b * BLK] == doc_ref[0, (b - 1) * BLK], first, b)
        bound_s[0, b] = first
    last = jnp.int32(blocks)
    for b in reversed(range(blocks)):
        if b < blocks - 1:
            last = jnp.where(doc_ref[0, b * BLK] == doc_ref[0, (b + 1) * BLK], last, b + 1)
        bound_s[1, b] = last

    def some_tiles(group, _):
        tiles = []
        for u in range(SIDE):
            t = group * SIDE + u
            bounds = [
                (bound_s[0, t * per_q + i], bound_s[1, t * per_q + i]) for i in range(per_q)
            ]
            q = q_s[pl.ds(pl.multiple_of(t * QT, QT), QT), :]
            tiles.append((t, q, bounds))
        chunks = functools.reduce(
            jnp.maximum, [b[-1][1] - b[0][0] for _, _, b in tiles]
        )
        big = (chunks + per_k // 2 - 1) // per_k
        small = jnp.where(chunks > big * per_k, 1, 0)

        def one_chunk(width, base, c, carry):
            result = []
            for (_, q, bounds), (high, total) in zip(tiles, carry):
                begin = bounds[0][0] + base + c * (width // BLK)
                keys = pl.ds(pl.multiple_of(jnp.minimum(begin, blocks) * BLK, BLK), width)
                scores = lax.dot_general(k_s[keys, :], q, NT, preferred_element_type=F32)
                columns = []
                for i, (lo, hi) in enumerate(bounds):
                    kept = [
                        jnp.where(
                            (begin + j >= lo) & (begin + j < hi),
                            scores[j * BLK : (j + 1) * BLK, i * BLK : (i + 1) * BLK],
                            -jnp.inf,
                        )
                        for j in range(width // BLK)
                    ]
                    columns.append(jnp.concatenate(kept, axis=0))
                scores = jnp.concatenate(columns, axis=1)
                newer = jnp.maximum(high, jnp.max(scores, axis=0, keepdims=True))
                expo = jnp.exp2(scores - newer).astype(BF)
                total = total * jnp.exp2(high - newer) + jnp.dot(
                    v_s[:, keys], expo, preferred_element_type=F32
                )
                result.append((newer, total))
            return tuple(result)

        carry = tuple(
            (jnp.full((1, QT), NEG, F32), jnp.zeros((VROWS, QT), F32)) for _ in range(SIDE)
        )
        carry = lax.fori_loop(0, big, functools.partial(one_chunk, KT, 0), carry)
        carry = lax.fori_loop(
            0, small, functools.partial(one_chunk, KT // 2, big * per_k), carry
        )
        for (t, _, _), (_, total) in zip(tiles, carry):
            o_s[:, pl.ds(pl.multiple_of(t * QT, QT), QT)] = total / total[HD : HD + 1, :]
        return 0

    lax.fori_loop(0, length // (QT * SIDE), some_tiles, 0)
    tok = length // n_seq
    for s in range(n_seq):
        mine = o_s[0:HD, s * tok : (s + 1) * tok]
        rest = mine[:, LANES:tok]
        out_ref[s, 0:64, :] = mine[0:64, 0:LANES].astype(BF)
        out_ref[s, 64:96, :] = jnp.concatenate([rest[0:32], rest[32:64]], axis=1).astype(BF)
        empty = jnp.zeros((HD - 64, 2 * LANES - tok), F32)
        out_ref[s, 96:112, :] = jnp.concatenate(
            [mine[64:HD, 0:LANES], jnp.concatenate([rest[64:HD], empty], axis=1)], axis=0
        ).astype(BF)


def project_kernel(n_seq, in_ref, w_ref, out_ref):
    width = out_ref.shape[1]
    tok = out_ref.shape[0]
    rest = tok - LANES
    lo = in_ref[:, 0:32, :].reshape(n_seq * 32, LANES)
    hi = in_ref[:, 32:64, :].reshape(n_seq * 32, LANES)
    far = in_ref[:, 64:96, :].reshape(n_seq * 32, LANES)
    tail = in_ref[:, 96:112, :].reshape(n_seq * 16, LANES).astype(F32)
    upper = (iota(tail.shape, 0) & 15) < 8
    tail_near = jnp.where(upper, tail, 0.0).astype(BF)
    tail_far = jnp.where(upper, 0.0, tail).astype(BF)
    near = jnp.concatenate([lo, hi, tail_near], axis=0).T
    far_t = far.T
    distant = jnp.concatenate([far_t[0:rest], far_t[rest:LANES], tail_far.T[0:rest]], axis=1)
    left = jnp.concatenate([near, distant], axis=0)
    last = w_ref[:, 64:HD, :].astype(F32)
    weights = jnp.concatenate(
        [
            w_ref[:, 0:32, :].reshape(n_seq * 32, width),
            w_ref[:, 32:64, :].reshape(n_seq * 32, width),
            jnp.concatenate([last, last], axis=1).reshape(n_seq * 16, width).astype(BF),
        ],
        axis=0,
    )
    out_ref[...] = jnp.dot(left, weights, preferred_element_type=F32).astype(BF)


def cost(flops, operands, out_shape):
    total = sum(math.prod(x.shape) * x.dtype.itemsize for x in operands)
    total += sum(math.prod(x.shape) * x.dtype.itemsize for x in jax.tree.leaves(out_shape))
    return pl.CostEstimate(flops=flops, bytes_accessed=total, transcendentals=0)


def local_call(kernel, out_shape, *operands, name, flops, small=0, scratch=(), behind=(), mib=30):
    smem = pl.BlockSpec(memory_space=pltpu.SMEM)
    vmem = pl.BlockSpec(memory_space=pltpu.VMEM)
    after = [pl.BlockSpec(memory_space=pl.ANY)] * len(behind)
    return pl.pallas_call(
        kernel,
        out_shape=out_shape,
        in_specs=[smem] * small + [vmem] * (len(operands) - small) + after,
        out_specs=jax.tree.map(lambda _: vmem, out_shape),
        scratch_shapes=scratch,
        compiler_params=pltpu.CompilerParams(vmem_limit_bytes=mib * 2**20),
        cost_estimate=cost(flops, operands, out_shape),
        name=name,
    )(*operands, *behind)


def project_qkv(blocks, mine_w, pair_w, name, behind=()):
    rows = sum(x.shape[0] for x in blocks)
    out = jax.ShapeDtypeStruct((rows // TOK, TOK, QKV), BF)
    flops = 2 * rows * mine_w.shape[1] * 6 * HD
    return local_call(
        functools.partial(qkv_kernel, len(blocks)),
        (out, out),
        *blocks,
        mine_w,
        pair_w,
        name=name,
        flops=flops,
        behind=behind,
    )


def attend_call(me, doc_ids, n_seq, *blocks):
    length = n_seq * TOK
    return local_call(
        functools.partial(attend_kernel, n_seq),
        jax.ShapeDtypeStruct((n_seq, AROWS, LANES), BF),
        me,
        doc_ids,
        *blocks,
        small=2,
        flops=2 * length * length * HD,
        scratch=[
            pltpu.VMEM((length, HD), BF),
            pltpu.VMEM((length + KT, HD), BF),
            pltpu.VMEM((length, LANES), BF),
            pltpu.VMEM((VROWS, length + KT), BF),
            pltpu.VMEM((VROWS, length), F32),
            pltpu.SMEM((2, length // BLK), jnp.int32),
        ],
        name="attend",
    )


def pick_kernel(me_ref, right_ref, left_ref, *refs):
    out_ref = refs[-1]

    @pl.when((me_ref[0] & 1) == 0)
    def _():
        out_ref[...] = right_ref[...]

    @pl.when((me_ref[0] & 1) == 1)
    def _():
        out_ref[...] = left_ref[...]


def ring_step(right, left, n_seq):
    up = [(i, (i + 2) % n_seq) for i in range(n_seq)]
    down = [(i, (i - 2) % n_seq) for i in range(n_seq)]
    return lax.ppermute(right, "seq", up), lax.ppermute(left, "seq", down)


def body(source, destination, doc_ids, w_qkv, w_out):
    n_pack = lax.axis_size("pack")
    n_seq = lax.axis_size("seq")
    width = source.shape[2]
    shape = jax.ShapeDtypeStruct
    me = lax.axis_index("seq").astype(jnp.int32).reshape(1)
    w_t = jnp.transpose(w_qkv, (0, 2, 1)).reshape(3 * HD, width)

    def other_core(x):
        return lax.ppermute(x, "seq", [(i, i ^ 1) for i in range(n_seq)])

    outbox = local_call(
        functools.partial(pack_kernel, n_pack),
        shape((n_pack, TILES * 16, LANES), BF),
        destination,
        source[0],
        name="pack_rows",
        flops=10**9,
        mib=56,
    )
    inbox = lax.all_to_all(outbox, "pack", split_axis=0, concat_axis=0, tiled=True)

    pair_w = other_core(w_t)
    w_all = lax.all_gather(w_out, "seq", axis=0, tiled=False)

    packed = local_call(
        functools.partial(unpack_kernel, n_pack),
        shape((TOK, width), BF),
        inbox,
        name="unpack_rows",
        flops=10**9,
        behind=(pair_w,),
    )
    right = left = packed
    held = [packed]
    for _ in range(3):
        right, left = ring_step(right, left, n_seq)
        held += [right, left]
    mine, theirs = project_qkv(
        held[:5], w_t, pair_w, "qkv_first", behind=(w_all[0, 0:16, 0:LANES],)
    )
    picked = local_call(
        pick_kernel,
        shape((TOK, width), BF),
        me,
        right,
        left,
        small=1,
        behind=(theirs,),
        name="pick",
        flops=0,
    )
    ways = [(i, (i + 2 - 4 * (i % 2)) % n_seq) for i in range(n_seq)]
    held.append(lax.ppermute(picked, "seq", ways))
    last_mine, last_theirs = project_qkv(held[5:], w_t, pair_w, "qkv_last")
    ours = [mine, last_mine, other_core(theirs), other_core(last_theirs)]
    attended = attend_call(me, doc_ids, n_seq, *ours)
    blocks = lax.all_to_all(attended, "seq", split_axis=0, concat_axis=0, tiled=True)

    out = local_call(
        functools.partial(project_kernel, n_seq),
        shape((TOK, width), BF),
        blocks,
        w_all,
        name="project",
        flops=2 * TOK * width * width,
    )
    return out[None]


def solution(mesh):
    placed = (
        P("seq", "pack", None),
        P("seq", "pack"),
        P("pack", None),
        P(None, None, "seq"),
        P("seq", None),
    )
    return jax.shard_map(
        body, mesh=mesh, in_specs=placed, out_specs=P("pack", "seq", None), check_vma=False
    )
```

```python
import functools
import math

import jax
import jax.numpy as jnp
from jax import lax
from jax.experimental import pallas as pl
from jax.experimental.pallas import tpu as pltpu
from jax.sharding import PartitionSpec as P

HD = 72
CAP = 12
LANES = 128
BLK = 128
BF = jnp.bfloat16
F32 = jnp.float32
NT = (((1,), (1,)), ((), ()))

SHIFTS = (
    (0, ((0, 0), (3, 4), (6, 8))),
    (-12, ((0, 1), (3, 5))),
    (4, ((1, 1), (4, 5))),
    (-8, ((1, 2), (4, 6))),
    (8, ((2, 2), (5, 6))),
    (-4, ((2, 3), (5, 7))),
)
TILES = 7


def iota(shape, dim):
    return lax.broadcasted_iota(jnp.int32, shape, dim)


def onehot(condition):
    return jnp.where(condition, 1.0, 0.0).astype(BF)


def pack_kernel(n_pack, dest_ref, rows_ref, out_ref):
    tok = rows_ref.shape[0]
    group = n_pack * 16
    dest = dest_ref[...]
    owner = ((dest >> 6) * 171) >> 9
    place = dest - owner * tok
    owned = iota((n_pack, tok), 0) == owner
    before = onehot(iota((tok, tok), 0) < iota((tok, tok), 1))
    counted = jnp.dot(onehot(owned), before, preferred_element_type=F32)
    slot = jnp.sum(jnp.where(owned, counted, 0.0), axis=0, keepdims=True).astype(jnp.int32)
    row = iota((group, tok), 0)
    parts = {}
    for shift, pairs in SHIFTS:
        at = slot - shift
        key = jnp.where((at >= 0) & (at < 16), owner * 16 + at, -1)
        picked = jnp.concatenate(
            [rows_ref[:, f * LANES : (f + 1) * LANES] for _, f in pairs], axis=1
        )
        moved = jnp.dot(onehot(row == key), picked, preferred_element_type=F32)
        for n, (tile, _) in enumerate(pairs):
            parts.setdefault(tile, []).append(moved[:, n * LANES : (n + 1) * LANES])
    tags = jnp.where(iota((LANES, tok), 0) == slot, (place + 1).astype(F32), 0.0).astype(BF)
    here = onehot(row == owner * 16 + CAP)
    parts[TILES - 1].append(lax.dot_general(here, tags, NT, preferred_element_type=F32))
    for tile in range(TILES):
        whole = functools.reduce(lambda a, b: a + b, parts[tile])
        out_ref[:, tile * 16 : (tile + 1) * 16, :] = whole.astype(BF).reshape(n_pack, 16, LANES)


def unpack_kernel(n_pack, in_ref, *refs):
    out_ref = refs[-1]
    tok = out_ref.shape[0]
    group = n_pack * 16
    tiles = [in_ref[:, t * 16 : (t + 1) * 16, :].reshape(group, LANES) for t in range(TILES)]
    col = iota((n_pack, group), 1)
    lead = iota((n_pack, group), 0) * 16
    labels = jnp.dot(onehot(col == lead + CAP), tiles[-1], preferred_element_type=F32).astype(BF)
    mine = (col >= lead) & (col < lead + 16)
    offset = iota((LANES, group), 0) - (iota((LANES, group), 1) & 15)
    place = iota((tok, group), 0) + 1
    parts = {}
    for shift, pairs in SHIFTS:
        spread = jnp.dot(labels, onehot(offset == shift), preferred_element_type=F32)
        label = jnp.sum(jnp.where(mine, spread, 0.0), axis=0, keepdims=True).astype(jnp.int32)
        picked = jnp.concatenate([tiles[t] for t, _ in pairs], axis=1)
        moved = jnp.dot(onehot(place == label), picked, preferred_element_type=F32)
        for n, (_, f) in enumerate(pairs):
            parts.setdefault(f, []).append(moved[:, n * LANES : (n + 1) * LANES])
    for f in sorted(parts):
        whole = functools.reduce(lambda a, b: a + b, parts[f])
        out_ref[:, f * LANES : (f + 1) * LANES] = whole.astype(BF)


TOK = 192
QT = 768
KT = 1536
SIDE = 1
VROWS = 80
QKV = 256
AROWS = 112
NEG = -3e38
BACK = (0, 1, -1, 2, -2, 3, -3, 4)


def origin(me, n):
    chips = len(BACK)
    core = me & 1
    chip = ((me >> 1) - BACK[n % chips]) & (chips - 1)
    return 2 * chip + (core if n < chips else 1 - core)


def qkv_kernel(count, *refs):
    x_refs = refs[:count]
    mine_w_ref, pair_w_ref = refs[count : count + 2]
    mine_ref, pair_ref = refs[-2:]
    x = jnp.concatenate([ref[...] for ref in x_refs], axis=0)
    rows = x.shape[0]
    scale = jnp.where(iota((1, 3 * HD), 1) < HD, math.log2(math.e) / math.sqrt(HD), 1.0)
    fill = jnp.where(iota((rows, QKV - 3 * HD), 1) < VROWS - HD, 1.0, 0.0)
    for w_ref, out_ref in ((mine_w_ref, mine_ref), (pair_w_ref, pair_ref)):
        qkv = lax.dot_general(x, w_ref[...], NT, preferred_element_type=F32) * scale
        whole = jnp.concatenate([qkv, fill], axis=1).astype(BF)
        out_ref[...] = whole.reshape(rows // TOK, TOK, QKV)


def attend_kernel(n_seq, me_ref, doc_ref, *refs):
    *in_refs, out_ref, q_s, k_s, row_s, v_s, o_s, bound_s = refs
    n = 0
    for ref in in_refs:
        for i in range(ref.shape[0]):
            rows = pl.ds(pl.multiple_of(origin(me_ref[0], n) * TOK, 64), TOK)
            q_s[rows, :] = ref[i, :, 0:HD]
            k_s[rows, :] = ref[i, :, HD : 2 * HD]
            row_s[rows, :] = ref[i, :, LANES:QKV]
            n += 1
    length = q_s.shape[0]
    blocks = length // BLK
    per_q = QT // BLK
    per_k = KT // BLK
    for b in range(blocks):
        turned = row_s[b * BLK : (b + 1) * BLK, :].T
        begin = 2 * HD - LANES
        v_s[:, b * BLK : (b + 1) * BLK] = turned[begin : begin + VROWS, :]
    k_s[length:, :] = jnp.zeros((KT, HD), BF)
    v_s[:, length:] = jnp.zeros((VROWS, KT), BF)
    first = jnp.int32(0)
    for b in range(blocks):
        if b:
            first = jnp.where(doc_ref[0, b * BLK] == doc_ref[0, (b - 1) * BLK], first, b)
        bound_s[0, b] = first
    last = jnp.int32(blocks)
    for b in reversed(range(blocks)):
        if b < blocks - 1:
            last = jnp.where(doc_ref[0, b * BLK] == doc_ref[0, (b + 1) * BLK], last, b + 1)
        bound_s[1, b] = last

    def some_tiles(group, _):
        tiles = []
        for u in range(SIDE):
            t = group * SIDE + u
            bounds = [
                (bound_s[0, t * per_q + i], bound_s[1, t * per_q + i]) for i in range(per_q)
            ]
            q = q_s[pl.ds(pl.multiple_of(t * QT, QT), QT), :]
            tiles.append((t, q, bounds))
        chunks = functools.reduce(
            jnp.maximum, [b[-1][1] - b[0][0] for _, _, b in tiles]
        )
        big = (chunks + per_k // 2 - 1) // per_k
        small = jnp.where(chunks > big * per_k, 1, 0)

        def one_chunk(width, base, c, carry):
            result = []
            for (_, q, bounds), (high, total) in zip(tiles, carry):
                begin = bounds[0][0] + base + c * (width // BLK)
                keys = pl.ds(pl.multiple_of(jnp.minimum(begin, blocks) * BLK, BLK), width)
                scores = lax.dot_general(k_s[keys, :], q, NT, preferred_element_type=F32)
                columns = []
                for i, (lo, hi) in enumerate(bounds):
                    kept = [
                        jnp.where(
                            (begin + j >= lo) & (begin + j < hi),
                            scores[j * BLK : (j + 1) * BLK, i * BLK : (i + 1) * BLK],
                            -jnp.inf,
                        )
                        for j in range(width // BLK)
                    ]
                    columns.append(jnp.concatenate(kept, axis=0))
                scores = jnp.concatenate(columns, axis=1)
                newer = jnp.maximum(high, jnp.max(scores, axis=0, keepdims=True))
                expo = jnp.exp2(scores - newer).astype(BF)
                total = total * jnp.exp2(high - newer) + jnp.dot(
                    v_s[:, keys], expo, preferred_element_type=F32
                )
                result.append((newer, total))
            return tuple(result)

        carry = tuple(
            (jnp.full((1, QT), NEG, F32), jnp.zeros((VROWS, QT), F32)) for _ in range(SIDE)
        )
        carry = lax.fori_loop(0, big, functools.partial(one_chunk, KT, 0), carry)
        carry = lax.fori_loop(
            0, small, functools.partial(one_chunk, KT // 2, big * per_k), carry
        )
        for (t, _, _), (_, total) in zip(tiles, carry):
            o_s[:, pl.ds(pl.multiple_of(t * QT, QT), QT)] = total / total[HD : HD + 1, :]
        return 0

    lax.fori_loop(0, length // (QT * SIDE), some_tiles, 0)
    tok = length // n_seq
    for s in range(n_seq):
        mine = o_s[0:HD, s * tok : (s + 1) * tok]
        rest = mine[:, LANES:tok]
        out_ref[s, 0:64, :] = mine[0:64, 0:LANES].astype(BF)
        out_ref[s, 64:96, :] = jnp.concatenate([rest[0:32], rest[32:64]], axis=1).astype(BF)
        empty = jnp.zeros((HD - 64, 2 * LANES - tok), F32)
        out_ref[s, 96:112, :] = jnp.concatenate(
            [mine[64:HD, 0:LANES], jnp.concatenate([rest[64:HD], empty], axis=1)], axis=0
        ).astype(BF)


def project_kernel(n_seq, in_ref, w_ref, out_ref):
    width = out_ref.shape[1]
    tok = out_ref.shape[0]
    rest = tok - LANES
    lo = in_ref[:, 0:32, :].reshape(n_seq * 32, LANES)
    hi = in_ref[:, 32:64, :].reshape(n_seq * 32, LANES)
    far = in_ref[:, 64:96, :].reshape(n_seq * 32, LANES)
    tail = in_ref[:, 96:112, :].reshape(n_seq * 16, LANES).astype(F32)
    upper = (iota(tail.shape, 0) & 15) < 8
    tail_near = jnp.where(upper, tail, 0.0).astype(BF)
    tail_far = jnp.where(upper, 0.0, tail).astype(BF)
    near = jnp.concatenate([lo, hi, tail_near], axis=0).T
    far_t = far.T
    distant = jnp.concatenate([far_t[0:rest], far_t[rest:LANES], tail_far.T[0:rest]], axis=1)
    left = jnp.concatenate([near, distant], axis=0)
    last = w_ref[:, 64:HD, :].astype(F32)
    weights = jnp.concatenate(
        [
            w_ref[:, 0:32, :].reshape(n_seq * 32, width),
            w_ref[:, 32:64, :].reshape(n_seq * 32, width),
            jnp.concatenate([last, last], axis=1).reshape(n_seq * 16, width).astype(BF),
        ],
        axis=0,
    )
    out_ref[...] = jnp.dot(left, weights, preferred_element_type=F32).astype(BF)


def cost(flops, operands, out_shape):
    total = sum(math.prod(x.shape) * x.dtype.itemsize for x in operands)
    total += sum(math.prod(x.shape) * x.dtype.itemsize for x in jax.tree.leaves(out_shape))
    return pl.CostEstimate(flops=flops, bytes_accessed=total, transcendentals=0)


def local_call(kernel, out_shape, *operands, name, flops, small=0, scratch=(), behind=(), mib=30):
    smem = pl.BlockSpec(memory_space=pltpu.SMEM)
    vmem = pl.BlockSpec(memory_space=pltpu.VMEM)
    after = [pl.BlockSpec(memory_space=pl.ANY)] * len(behind)
    return pl.pallas_call(
        kernel,
        out_shape=out_shape,
        in_specs=[smem] * small + [vmem] * (len(operands) - small) + after,
        out_specs=jax.tree.map(lambda _: vmem, out_shape),
        scratch_shapes=scratch,
        compiler_params=pltpu.CompilerParams(vmem_limit_bytes=mib * 2**20),
        cost_estimate=cost(flops, operands, out_shape),
        name=name,
    )(*operands, *behind)


def project_qkv(blocks, mine_w, pair_w, name, behind=()):
    rows = sum(x.shape[0] for x in blocks)
    out = jax.ShapeDtypeStruct((rows // TOK, TOK, QKV), BF)
    flops = 2 * rows * mine_w.shape[1] * 6 * HD
    return local_call(
        functools.partial(qkv_kernel, len(blocks)),
        (out, out),
        *blocks,
        mine_w,
        pair_w,
        name=name,
        flops=flops,
        behind=behind,
    )


def attend_call(me, doc_ids, n_seq, *blocks):
    length = n_seq * TOK
    return local_call(
        functools.partial(attend_kernel, n_seq),
        jax.ShapeDtypeStruct((n_seq, AROWS, LANES), BF),
        me,
        doc_ids,
        *blocks,
        small=2,
        flops=2 * length * length * HD,
        scratch=[
            pltpu.VMEM((length, HD), BF),
            pltpu.VMEM((length + KT, HD), BF),
            pltpu.VMEM((length, LANES), BF),
            pltpu.VMEM((VROWS, length + KT), BF),
            pltpu.VMEM((VROWS, length), F32),
            pltpu.SMEM((2, length // BLK), jnp.int32),
        ],
        name="attend",
    )


def pick_kernel(me_ref, right_ref, left_ref, *refs):
    out_ref = refs[-1]

    @pl.when((me_ref[0] & 1) == 0)
    def _():
        out_ref[...] = right_ref[...]

    @pl.when((me_ref[0] & 1) == 1)
    def _():
        out_ref[...] = left_ref[...]


def ring_step(right, left, n_seq):
    up = [(i, (i + 2) % n_seq) for i in range(n_seq)]
    down = [(i, (i - 2) % n_seq) for i in range(n_seq)]
    return lax.ppermute(right, "seq", up), lax.ppermute(left, "seq", down)


def body(source, destination, doc_ids, w_qkv, w_out):
    n_pack = lax.axis_size("pack")
    n_seq = lax.axis_size("seq")
    width = source.shape[2]
    shape = jax.ShapeDtypeStruct
    me = lax.axis_index("seq").astype(jnp.int32).reshape(1)
    w_t = jnp.transpose(w_qkv, (0, 2, 1)).reshape(3 * HD, width)

    def other_core(x):
        return lax.ppermute(x, "seq", [(i, i ^ 1) for i in range(n_seq)])

    outbox = local_call(
        functools.partial(pack_kernel, n_pack),
        shape((n_pack, TILES * 16, LANES), BF),
        destination,
        source[0],
        name="pack_rows",
        flops=10**9,
        mib=56,
    )
    inbox = lax.all_to_all(outbox, "pack", split_axis=0, concat_axis=0, tiled=True)

    pair_w = other_core(w_t)
    w_all = lax.all_gather(w_out, "seq", axis=0, tiled=False)

    packed = local_call(
        functools.partial(unpack_kernel, n_pack),
        shape((TOK, width), BF),
        inbox,
        name="unpack_rows",
        flops=10**9,
        behind=(pair_w,),
    )
    right = left = packed
    held = [packed]
    for _ in range(3):
        right, left = ring_step(right, left, n_seq)
        held += [right, left]
    mine, theirs = project_qkv(
        held[:5], w_t, pair_w, "qkv_first", behind=(w_all[0, 0:16, 0:LANES],)
    )
    picked = local_call(
        pick_kernel,
        shape((TOK, width), BF),
        me,
        right,
        left,
        small=1,
        behind=(theirs,),
        name="pick",
        flops=0,
    )
    ways = [(i, (i + 2 - 4 * (i % 2)) % n_seq) for i in range(n_seq)]
    held.append(lax.ppermute(picked, "seq", ways))
    last_mine, last_theirs = project_qkv(held[5:], w_t, pair_w, "qkv_last")
    ours = [mine, last_mine, other_core(theirs), other_core(last_theirs)]
    attended = attend_call(me, doc_ids, n_seq, *ours)
    blocks = lax.all_to_all(attended, "seq", split_axis=0, concat_axis=0, tiled=True)

    out = local_call(
        functools.partial(project_kernel, n_seq),
        shape((TOK, width), BF),
        blocks,
        w_all,
        name="project",
        flops=2 * TOK * width * width,
    )
    return out[None]


def solution(mesh):
    placed = (
        P("seq", "pack", None),
        P("seq", "pack"),
        P("pack", None),
        P(None, None, "seq"),
        P("seq", None),
    )
    return jax.shard_map(
        body, mesh=mesh, in_specs=placed, out_specs=P("pack", "seq", None), check_vma=False
    )
```
